32 devices in a mesh: dp: 16 (over z, y, core), tensor: 2 (over x).
Axes of the slice: x: 2, y: 2, z: 4, core: 2. Of those that a mesh axis runs over, the one named last changes fastest.
Arguments:
- tokens: bfloat16 [8192, 768], P('dp'), may hold values from -6 to 6
- seg_ids: int32 [8192], P('dp'), may hold values from 0 to 2, as said below
- positions: int32 [8192], P('dp'), may hold values from 0 to 382, as said below
- gain_attn: bfloat16 [768], P('dp'), may hold values from 0.25 to 1.75
- w_qkv: bfloat16 [768, 3, 768], P('dp', None, 'tensor'), may hold values from -0.21875 to 0.21875
- w_attn_out: bfloat16 [768, 768], P('tensor', 'dp'), may hold values from -1.75 to 1.75
- gain_mlp: bfloat16 [768], P('dp'), may hold values from 0.25 to 1.75
- w_in: bfloat16 [768, 2, 1152], P('dp', None, 'tensor'), may hold values from -0.21875 to 0.21875
- w_mlp_out: bfloat16 [1152, 768], P('tensor', 'dp'), may hold values from -0.375 to 0.375
- cotangent: bfloat16 [8192, 768], P('dp'), may hold values from -8 to 8
Outputs:
- output: bfloat16 [8192, 768], P('dp')
- grad_input: float32 [8192, 768], P('dp')
- grad_gain_attn: float32 [768], P('dp')
- grad_qkv: float32 [768, 3, 768], P('dp', None, 'tensor')
- grad_attn_out: float32 [768, 768], P('tensor', 'dp')
- grad_gain_mlp: float32 [768], P('dp')
- grad_in: float32 [768, 2, 1152], P('dp', None, 'tensor')
- grad_mlp_out: float32 [1152, 768], P('tensor', 'dp')
The draws below stay inside these ranges and needn't reach their ends.
Inputs may be any that keep to these rules, and one draw needn't show every extreme that they name: `seg_ids`: within each aligned run of 512 tokens (one sequence) the ids never fall and take each of 0, 1 and 2 once as a run; the document numbered 1 contains the tokens 512 / 2 - 1 and 256 of its sequence. `positions`: 0 at the first token of each sequence and wherever seg_ids changes, else one more than at the token before; some document is 383 tokens long, and none is longer.
All inputs are finite; a program needn't handle non-finite values.
Results may differ from the reference program's by a relative error of at most 0.019.
Values may be sent and summed in bfloat16 or wider, within the bound.
No kernel may reach another device: no remote copies, remote signals or barrier semaphores. Data moves between devices by JAX's collectives and lax.ppermute only.
A program may use at most 128 MiB of HBM per device.

```python
import jax
import jax.numpy as jnp
from jax import lax

D = 768
HEADS = 12
HD = 64
FF = 1152
HALF = 64
LEN = 512
TOKENS = 8192


def document_bounds(key):
    sequences = TOKENS // LEN
    first = jax.random.randint(key, (sequences, 1), LEN // 8, 3 * LEN // 8)
    second = jax.random.randint(jax.random.fold_in(key, 1), (sequences, 1), 5 * LEN // 8, 7 * LEN // 8)
    chosen = jax.random.randint(jax.random.fold_in(key, 2), (), 0, sequences)
    picked = jnp.arange(sequences, dtype=jnp.int32)[:, None] == chosen
    first = jnp.where(picked, LEN // 8, first)
    second = jnp.where(picked, 7 * LEN // 8 - 1, second)
    index = jnp.arange(LEN, dtype=jnp.int32)[None, :]
    return (first, second, index)


def draw_seg_ids(key, part):
    first, second, index = document_bounds(key)
    number = (index >= first).astype(jnp.int32) + (index >= second).astype(jnp.int32)
    return number.reshape(TOKENS)


def draw_positions(key, part):
    first, second, index = document_bounds(key)
    begin = jnp.where(index >= second, second, jnp.where(index >= first, first, 0))
    return (index - begin).astype(jnp.int32).reshape(TOKENS)


def with_spikes(values, key, source, target, blocks, factor):
    def block_of(axis_at):
        return (jnp.arange(values.shape[axis_at]) // (values.shape[axis_at] // blocks)).reshape((-1,) + (1,) * (values.ndim - 1 - axis_at))

    first = jax.random.permutation(key, blocks)[block_of(target)]
    far = (block_of(target) + blocks // 2) % blocks
    return jnp.where((block_of(source) == first) | (block_of(source) == far), factor * values, values)


def level_of(stream_key, dims, split, smallest, largest):
    factor_of = 1.0
    for dim, blocks in split:
        steps = jax.random.uniform(jax.random.fold_in(jax.random.fold_in(stream_key, 6), dim), (blocks,), jnp.float32, smallest / len(split), largest / len(split))
        factor_of = factor_of * jnp.repeat(jnp.exp(steps), dims[dim] // blocks).reshape((-1,) + (1,) * (len(dims) - 1 - dim))
    return factor_of


def scatter_about(stream_key, dims, width, most, cuts=(), kind=jnp.bfloat16):
    level = level_of(stream_key, dims, cuts, -0.22, 0.18) if cuts else 1.0
    entries = jax.random.normal(stream_key, dims, jnp.float32) * width * level
    return jnp.minimum(jnp.maximum(entries, -most), most).astype(kind)


def noise_with(key, dims, width, reach, pieces, heavy, held_as=jnp.bfloat16):
    drawn = width * jax.random.normal(key, dims, jnp.float32)
    if pieces:
        drawn = drawn * level_of(key, dims, pieces, -0.22, 0.18)
    return jnp.clip(with_spikes(drawn, jax.random.fold_in(key, 3), *heavy), -reach, reach).astype(held_as)


def setup_inputs(seed: int = 0) -> dict:
    key_of = jax.random.split(jax.random.key(seed), 11)
    tokens = scatter_about(key_of[0], (TOKENS, D), 1.0, 6.0, ((0, 16),))
    seg_ids = draw_seg_ids(jax.random.fold_in(key_of[10], 71), 0)
    positions = draw_positions(jax.random.fold_in(key_of[10], 71), 0)
    gain_attn = jnp.clip(1.0 + 0.15 * jax.random.normal(key_of[3], (D,), jnp.float32), 0.25, 1.75).astype(jnp.bfloat16)
    w_qkv = scatter_about(key_of[4], (D, 3, HEADS * HD), D ** -0.5, 0.21875, ((0, 16), (2, 2)))
    w_attn_out = scatter_about(key_of[5], (HEADS * HD, D), (HEADS * HD // 64) ** -0.5, 1.75, ((0, 2), (1, 16)))
    gain_mlp = jnp.clip(1.0 + 0.15 * jax.random.normal(key_of[6], (D,), jnp.float32), 0.25, 1.75).astype(jnp.bfloat16)
    w_in = scatter_about(key_of[7], (D, 2, FF), D ** -0.5, 0.21875, ((0, 16), (2, 2)))
    w_mlp_out = scatter_about(key_of[8], (FF, D), (FF // 4) ** -0.5, 0.375, ((0, 2), (1, 16)))
    cotangent = noise_with(key_of[9], (TOKENS, D), 1.0, 8.0, ((0, 16),), (0, 1, 16, 2.0))
    return {"tokens": tokens, "seg_ids": seg_ids, "positions": positions, "gain_attn": gain_attn, "w_qkv": w_qkv, "w_attn_out": w_attn_out, "gain_mlp": gain_mlp, "w_in": w_in, "w_mlp_out": w_mlp_out, "cotangent": cotangent}


@jax.custom_vjp
def low(v):
    return lax.optimization_barrier(v.astype(jnp.bfloat16)).astype(jnp.float32)

@jax.custom_vjp
def low_back(v):
    return v

def low_keep(v):
    return (low(v), None)

def low_pass(kept, grad):
    return (grad,)

def back_keep(v):
    return (v, None)

def back_low(kept, grad):
    return (low(grad),)
low.defvjp(low_keep, low_pass)
low_back.defvjp(back_keep, back_low)
EPSILON = 1e-05
THETA = 10000.0
MASKED = -1e+30
HIGHEST = lax.Precision.HIGHEST

def layer_norm(values, gain):
    average = lax.optimization_barrier(jnp.mean(values, axis=-1, keepdims=True))
    centered = values - average
    variance = lax.optimization_barrier(jnp.mean(centered * centered, axis=-1, keepdims=True))
    return centered * lax.rsqrt(variance + EPSILON) * gain

def rope_tables(positions):
    frequency = THETA ** (-jnp.arange(0, HD, 2).astype(jnp.float32) / HD)
    angle = positions.astype(jnp.float32)[:, None] * frequency[None, :]
    angle = jnp.concatenate([angle, angle], axis=-1)
    return (jnp.cos(angle)[:, None, :], jnp.sin(angle)[:, None, :])

def rotate_half(values):
    middle = values.shape[-1] // 2
    return jnp.concatenate([-values[..., middle:], values[..., :middle]], axis=-1)

def rotate(values, cosine, sine):
    return values * cosine + rotate_half(values) * sine

def attend(query, keys, values, segments):
    block = min(512, LEN)
    span = block + 2 * HALF
    scale = HD ** (-0.5)
    wide_keys = jnp.pad(keys, ((HALF, HALF), (0, 0), (0, 0)))
    wide_values = jnp.pad(values, ((HALF, HALF), (0, 0), (0, 0)))
    wide_segments = jnp.pad(segments, (HALF, HALF), constant_values=-1)
    offsets = jnp.arange(span)[None, :] - HALF - jnp.arange(block)[:, None]
    near = jnp.abs(offsets) <= HALF

    def one_block(start):
        query_block = lax.dynamic_slice_in_dim(query, start, block, 0)
        key_block = lax.dynamic_slice_in_dim(wide_keys, start, span, 0)
        value_block = lax.dynamic_slice_in_dim(wide_values, start, span, 0)
        own_segments = lax.dynamic_slice_in_dim(segments, start, block, 0)
        key_segments = lax.dynamic_slice_in_dim(wide_segments, start, span, 0)
        allowed = near & (own_segments[:, None] == key_segments[None, :])
        scores = low_back(jnp.einsum('qhd,khd->hqk', query_block, key_block, precision=HIGHEST) * scale)
        scores = jnp.where(allowed[None], scores, MASKED)
        shares = low(jax.nn.softmax(scores, axis=-1))
        return jnp.einsum('hqk,khd->qhd', shares, value_block, precision=HIGHEST)
    starts = (jnp.arange(LEN // block) * block).astype(jnp.int32)
    blocks = lax.map(jax.checkpoint(one_block), starts)
    return blocks.reshape(LEN, HEADS, HD)

def forward(inputs, gain_attn, w_qkv, w_attn_out, gain_mlp, w_in, w_mlp_out, segments, positions):
    rows = inputs.shape[0]
    lowered_one = low(layer_norm(inputs, gain_attn))
    projected = jnp.dot(lowered_one, w_qkv.reshape(D, 3 * HEADS * HD), precision=HIGHEST)
    projected = projected.reshape(rows, 3, HEADS, HD)
    cosine, sine = rope_tables(positions)
    query = low(rotate(low_back(projected[:, 0]), cosine, sine))
    keys = low(rotate(low_back(projected[:, 1]), cosine, sine))
    values = low(low_back(projected[:, 2]))
    shape = (rows // LEN, LEN, HEADS, HD)
    context = jax.vmap(attend)(query.reshape(shape), keys.reshape(shape), values.reshape(shape), segments.reshape(rows // LEN, LEN))
    context = low(low_back(context.reshape(rows, HEADS * HD)))
    branch = low_back(jnp.dot(context, w_attn_out, precision=HIGHEST))
    middle = inputs + branch
    lowered_two = low(layer_norm(middle, gain_mlp))
    gates = jnp.dot(lowered_two, w_in.reshape(D, 2 * FF), precision=HIGHEST).reshape(rows, 2, FF)
    active = low_back(gates[:, 0])
    factor = low_back(gates[:, 1])
    mixed = low(jax.nn.gelu(active, approximate=False) * factor)
    return middle + low_back(jnp.dot(mixed, w_mlp_out, precision=HIGHEST))

def reference(tokens, seg_ids, positions, gain_attn, w_qkv, w_attn_out, gain_mlp, w_in, w_mlp_out, cotangent):
    sequences = TOKENS // LEN
    allowed_count = max(1, 4096 // LEN)
    group = 1
    for candidate in range(1, sequences + 1):
        if sequences % candidate == 0 and candidate <= allowed_count:
            group = candidate
    turns = sequences // group
    weights = (gain_attn.astype(jnp.float32), w_qkv.astype(jnp.float32), w_attn_out.astype(jnp.float32), gain_mlp.astype(jnp.float32), w_in.astype(jnp.float32), w_mlp_out.astype(jnp.float32))
    inputs = tokens.astype(jnp.float32).reshape(turns, group * LEN, D)
    segments = seg_ids.reshape(turns, group * LEN)
    places = positions.reshape(turns, group * LEN)
    upstream = cotangent.astype(jnp.float32).reshape(turns, group * LEN, D)

    def one_turn(carry, item):
        values, segment_part, place_part, grad_part = item

        def layer(values_in, gain_one, qkv_weight, out_weight, gain_two, in_weight, down_weight):
            return forward(values_in, gain_one, qkv_weight, out_weight, gain_two, in_weight, down_weight, segment_part, place_part)
        result, pull = jax.vjp(layer, values, *weights)
        grads = pull(grad_part)
        carry = tuple((total + grad for total, grad in zip(carry, grads[1:])))
        return (carry, (result.astype(jnp.bfloat16), grads[0]))
    start = tuple((jnp.zeros_like(weight) for weight in weights))
    totals, (results, grad_values) = lax.scan(one_turn, start, (inputs, segments, places, upstream))
    return (results.reshape(TOKENS, D), grad_values.reshape(TOKENS, D), totals[0], totals[1], totals[2], totals[3], totals[4], totals[5])
```

```python
import functools

import jax
import jax.numpy as jnp
from jax import lax
from jax.sharding import PartitionSpec as P

HD = 64
HALF = 64


EPSILON = 1e-05
THETA = 10000.0
MASKED = -1e30


def normalize(values):
    average = jnp.mean(values, axis=-1, keepdims=True)
    centered = values - average
    variance = jnp.mean(centered * centered, axis=-1, keepdims=True)
    inverse = lax.rsqrt(variance + EPSILON)
    return (centered * inverse, inverse)


def rope_tables(positions, size):
    frequency = THETA ** (-jnp.arange(0, size, 2).astype(jnp.float32) / size)
    angle = positions.astype(jnp.float32)[:, None] * frequency[None, :]
    angle = jnp.concatenate([angle, angle], axis=-1)
    return (jnp.cos(angle)[:, None, :], jnp.sin(angle)[:, None, :])


def rotate_half(values):
    middle = values.shape[-1] // 2
    return jnp.concatenate([-values[..., middle:], values[..., :middle]], axis=-1)


def rotate(values, cosine, sine):
    return values * cosine + rotate_half(values) * sine


def rotate_back(values, cosine, sine):
    return values * cosine - rotate_half(values * sine)


def gated(active, factor):
    return jax.nn.gelu(active, approximate=False) * factor


def levels_of(count):
    levels, stride = [], count
    while stride > 1:
        size = 4 if stride % 8 == 0 else 2 if stride % 2 == 0 else stride
        stride //= size
        levels.append((stride, size))
    return levels


def shifted(values, count, level, step):
    stride, size = level
    pairs = []
    for device in range(count):
        digit = (device // stride) % size
        pairs.append((device, device + ((digit + step) % size - digit) * stride))
    return lax.ppermute(values, "dp", pairs)


def gather_rows(shard, count):
    held = shard
    for level in levels_of(count):
        held = jnp.concatenate(
            [held] + [shifted(held, count, level, step) for step in range(1, level[1])], axis=0
        )
    return held


def scatter_rows(partial, count):
    held = partial
    for level in reversed(levels_of(count)):
        size = level[1]
        pieces = held.reshape(size, held.shape[0] // size, held.shape[1])
        total = pieces[0].astype(jnp.float32)
        for step in range(1, size):
            total = total + shifted(pieces[step], count, level, -step).astype(jnp.float32)
        held = lax.optimization_barrier(total.astype(jnp.bfloat16)) if level[0] != levels_of(count)[0][0] else total
    return held


def placement(count, width):
    device = lax.axis_index("dp")
    place = jnp.arange(count)
    owner, weight = jnp.zeros_like(place), 1
    for stride, size in levels_of(count):
        step = (place // weight) % size
        owner = owner + ((device // stride) % size - step + size) % size * stride
        weight *= size
    rows = width // count
    natural = (owner[:, None] * rows + jnp.arange(rows)[None, :]).reshape(width)
    return (natural[None, :] == jnp.arange(width)[:, None]).astype(jnp.bfloat16)


def reorder(values, matrix):
    return jnp.dot(values, matrix, preferred_element_type=jnp.float32)


def restore(values, matrix):
    return lax.dot_general(values, matrix, (((1,), (1,)), ((), ())), preferred_element_type=jnp.float32)


def pair_sum(part):
    own = lax.optimization_barrier(part.astype(jnp.bfloat16))
    other = lax.ppermute(own, "tensor", [(0, 1), (1, 0)])
    return own.astype(jnp.float32) + other.astype(jnp.float32)


def norm_back_scaled(scaled, normed, inverse):
    first = jnp.mean(scaled, axis=-1, keepdims=True)
    second = jnp.mean(scaled * normed, axis=-1, keepdims=True)
    return inverse * (scaled - first - normed * second)


def per_device(
    devices, tokens, seg_ids, positions, gain_attn, w_qkv, w_attn_out, gain_mlp, w_in, w_mlp_out, cotangent
):
    count = tokens.shape[0]
    width = tokens.shape[1]
    inner = w_qkv.shape[2]
    heads_here = inner // HD
    hidden = w_in.shape[2]
    rows = w_qkv.shape[0]
    gain_one = gain_attn.astype(jnp.float32)
    gain_two = gain_mlp.astype(jnp.float32)
    scaled_qkv = (w_qkv.astype(jnp.float32) * gain_one[:, None, None]).astype(jnp.bfloat16)
    scaled_in = (w_in.astype(jnp.float32) * gain_two[:, None, None]).astype(jnp.bfloat16)
    matrix_q, matrix_k, matrix_v = (gather_rows(scaled_qkv[:, i], devices) for i in range(3))
    matrix_qkv = jnp.concatenate([matrix_q, matrix_k, matrix_v], axis=1)
    rest = jnp.concatenate([w_attn_out.T, w_mlp_out.T, scaled_in.reshape(rows, 2 * hidden)], axis=1)
    rest = gather_rows(rest, devices)
    out_rows, down_rows, matrix_in = jnp.split(rest, [inner, inner + hidden], axis=1)

    order = placement(devices, width)
    inputs = reorder(tokens, order)
    upstream = reorder(cotangent, order).astype(jnp.bfloat16)
    normed_one, inverse_one = normalize(inputs)
    lowered_one = normed_one.astype(jnp.bfloat16)
    projected = jnp.dot(lowered_one, matrix_qkv, preferred_element_type=jnp.float32)
    projected = projected.reshape(count, 3, heads_here, HD)
    cosine, sine = rope_tables(positions, HD)
    query = rotate(projected[:, 0], cosine, sine).astype(jnp.bfloat16)
    keys = rotate(projected[:, 1], cosine, sine).astype(jnp.bfloat16)
    values = projected[:, 2].astype(jnp.bfloat16)
    wide_keys = jnp.pad(keys, ((HALF, HALF), (0, 0), (0, 0)))
    wide_values = jnp.pad(values, ((HALF, HALF), (0, 0), (0, 0)))
    wide_segments = jnp.pad(seg_ids, (HALF, HALF), constant_values=-1)
    block = min(512, count)
    span = block + 2 * HALF
    scale = HD ** (-0.5)
    offsets = jnp.arange(span)[None, :] - HALF - jnp.arange(block)[:, None]
    near = jnp.abs(offsets) <= HALF

    def scores_of():
        allowed = near & (seg_ids[:, None] == wide_segments[None, :])
        scores = (
            jnp.einsum("qhd,khd->hqk", query, wide_keys, preferred_element_type=jnp.float32) * scale
        )
        return (jnp.where(allowed[None], scores, MASKED), allowed)

    start = 0
    scores, allowed = scores_of()
    peak = jnp.max(scores, axis=-1, keepdims=True)
    powers = jnp.exp(scores - peak)
    total = jnp.sum(powers, axis=-1, keepdims=True)
    shares = (powers / total).astype(jnp.bfloat16)
    log_sums = [peak + jnp.log(total)]
    contexts = jnp.einsum("hqk,khd->qhd", shares, wide_values, preferred_element_type=jnp.float32)
    context = contexts.astype(jnp.bfloat16).reshape(count, inner)
    attn_part = lax.dot_general(context, out_rows, (((1,), (1,)), ((), ())), preferred_element_type=jnp.float32)
    middle = inputs + pair_sum(attn_part)
    normed_two, inverse_two = normalize(middle)
    lowered_two = normed_two.astype(jnp.bfloat16)
    gates = jnp.dot(lowered_two, matrix_in, preferred_element_type=jnp.float32)
    active, factor = gates[:, :hidden], gates[:, hidden:]
    mixed = gated(active, factor).astype(jnp.bfloat16)
    mlp_part = lax.dot_general(mixed, down_rows, (((1,), (1,)), ((), ())), preferred_element_type=jnp.float32)
    output = (middle + pair_sum(mlp_part)).astype(jnp.bfloat16)
    output = restore(output, order).astype(jnp.bfloat16)
    grad_down = jnp.dot(upstream.T, mixed, preferred_element_type=jnp.float32)
    grad_mixed = jnp.dot(upstream, down_rows, preferred_element_type=jnp.float32)
    unused, pull = jax.vjp(gated, active, factor)
    grad_active, grad_factor = pull(grad_mixed)
    grad_gates = jnp.concatenate([grad_active, grad_factor], axis=1).astype(jnp.bfloat16)
    grad_in = jnp.dot(lowered_two.T, grad_gates, preferred_element_type=jnp.float32)
    mlp_grads = jnp.concatenate([grad_down, grad_in], axis=1).astype(jnp.bfloat16)
    mlp_grads = scatter_rows(mlp_grads, devices)
    partial_two = lax.dot_general(grad_gates, matrix_in, (((1,), (1,)), ((), ())), preferred_element_type=jnp.float32)
    grad_middle = upstream.astype(jnp.float32) + norm_back_scaled(pair_sum(partial_two), normed_two, inverse_two)
    grad_branch = grad_middle.astype(jnp.bfloat16)
    grad_out = jnp.dot(grad_branch.T, context, preferred_element_type=jnp.float32).astype(jnp.bfloat16)
    grad_out = scatter_rows(grad_out, devices)
    grad_context = jnp.dot(grad_branch, out_rows, preferred_element_type=jnp.float32)
    grad_context = grad_context.astype(jnp.bfloat16).reshape(count, heads_here, HD)
    query_grads = []
    grad_keys = jnp.zeros((count + 2 * HALF, heads_here, HD), jnp.float32)
    grad_values = jnp.zeros((count + 2 * HALF, heads_here, HD), jnp.float32)
    for number, start in enumerate(range(0, count, block)):
        scores, allowed = scores_of()
        shares = jnp.where(allowed[None], jnp.exp(scores - log_sums[number]), 0.0)
        grad_shares = jnp.einsum(
            "qhd,khd->hqk", grad_context, wide_values, preferred_element_type=jnp.float32
        )
        grad_values = grad_values.at[start : start + span].add(
            jnp.einsum(
                "hqk,qhd->khd",
                shares.astype(jnp.bfloat16),
                grad_context,
                preferred_element_type=jnp.float32,
            )
        )
        row_sums = jnp.sum(shares * grad_shares, axis=-1, keepdims=True)
        grad_scores = (shares * (grad_shares - row_sums)).astype(jnp.bfloat16)
        query_grads.append(
            jnp.einsum("hqk,khd->qhd", grad_scores, wide_keys, preferred_element_type=jnp.float32)
            * scale
        )
        grad_keys = grad_keys.at[start : start + span].add(
            jnp.einsum("hqk,qhd->khd", grad_scores, query, preferred_element_type=jnp.float32)
            * scale
        )
    grad_query = rotate_back(query_grads[0], cosine, sine)
    grad_key_pre = rotate_back(grad_keys[HALF : HALF + count], cosine, sine)
    grad_projected = (
        jnp.stack(
            [
                grad_query.reshape(count, inner),
                grad_key_pre.reshape(count, inner),
                grad_values[HALF : HALF + count].reshape(count, inner),
            ],
            axis=1,
        )
        .astype(jnp.bfloat16)
        .reshape(count, 3 * inner)
    )
    grad_qkv = jnp.dot(lowered_one.T, grad_projected, preferred_element_type=jnp.float32).astype(jnp.bfloat16)
    grad_qkv = jnp.concatenate([scatter_rows(part, devices) for part in jnp.split(grad_qkv, 3, axis=1)], axis=1)
    partial_one = lax.dot_general(grad_projected, matrix_qkv, (((1,), (1,)), ((), ())), preferred_element_type=jnp.float32)
    grad_input = grad_middle + norm_back_scaled(pair_sum(partial_one), normed_one, inverse_one)
    high = lax.optimization_barrier(grad_input.astype(jnp.bfloat16))
    low = (grad_input - high.astype(jnp.float32)).astype(jnp.bfloat16)
    grad_input = restore(high, order) + restore(low, order)

    sum_qkv = grad_qkv.reshape(rows, 3, inner)
    sum_down = mlp_grads[:, :hidden]
    sum_in = mlp_grads[:, hidden:].reshape(rows, 2, hidden)
    gains = jnp.stack(
        [
            jnp.sum(w_qkv.astype(jnp.float32) * sum_qkv, axis=(1, 2)),
            jnp.sum(w_in.astype(jnp.float32) * sum_in, axis=(1, 2)),
        ]
    )
    gains = gains + lax.ppermute(gains, "tensor", [(0, 1), (1, 0)])
    return (
        output,
        grad_input,
        gains[0],
        sum_qkv * gain_one[:, None, None],
        grad_out.T,
        gains[1],
        sum_in * gain_two[:, None, None],
        sum_down.T,
    )


def solution(mesh):
    return jax.shard_map(
        functools.partial(per_device, mesh.shape["dp"]),
        mesh=mesh,
        in_specs=(
            P("dp", None),
            P("dp"),
            P("dp"),
            P("dp"),
            P("dp", None, "tensor"),
            P("tensor", "dp"),
            P("dp"),
            P("dp", None, "tensor"),
            P("tensor", "dp"),
            P("dp", None),
        ),
        out_specs=(
            P("dp", None),
            P("dp", None),
            P("dp"),
            P("dp", None, "tensor"),
            P("tensor", "dp"),
            P("dp"),
            P("dp", None, "tensor"),
            P("tensor", "dp"),
        ),
        check_vma=False,
    )
```

```python
import functools

import jax
import jax.numpy as jnp
from jax import lax
from jax.experimental import pallas as pl
from jax.experimental.pallas import tpu as pltpu
from jax.sharding import PartitionSpec as P

HD = 64
HALF = 64
LANES = 128
BLOCK = 128
WINDOW = 256
CHUNKS = 2
PIECES = 4

EPSILON = 1e-05
THETA = 10000.0
MASKED = -1e30
SCALE = HD ** (-0.5)

NN = (((1,), (0,)), ((), ()))
NT = (((1,), (1,)), ((), ()))
TN = (((0,), (0,)), ((), ()))


def product(left, right, dims=NN):
    return lax.dot_general(left, right, dims, preferred_element_type=jnp.float32)


def low(values):
    return values.astype(jnp.bfloat16)


def wide(values):
    return values.astype(jnp.float32)


def levels_of(count):
    levels, stride = [], count
    while stride > 1:
        size = 4 if stride % 8 == 0 else 2 if stride % 2 == 0 else stride
        stride //= size
        levels.append((stride, size))
    return levels


def shifted(values, count, level, step):
    stride, size = level
    pairs = []
    for device in range(count):
        digit = (device // stride) % size
        pairs.append((device, device + ((digit + step) % size - digit) * stride))
    return lax.ppermute(values, "dp", pairs)


def swapped(values):
    return lax.ppermute(values, "tensor", [(0, 1), (1, 0)])


def is_plain(count, rows):
    return levels_of(count) == [(4, 4), (2, 2), (1, 2)] and rows % 16 == 0


def gather_rows(shard, count):
    levels = levels_of(count)
    if is_plain(count, shard.shape[0]):
        first, second, third = levels
        held = stack_rows([shard] + [shifted(shard, count, first, step) for step in range(1, 4)])
        other = shifted(held, count, second, 1)
        return [held, other, shifted(held, count, third, 1), shifted(other, count, third, 1)]
    held = shard
    for level in levels:
        held = jnp.concatenate(
            [held] + [shifted(held, count, level, step) for step in range(1, level[1])], axis=0
        )
    return jnp.split(held, PIECES, axis=0)


def scatter_rows(kept, sent, count, rows):
    levels = levels_of(count)
    if is_plain(count, rows):
        first, second, third = levels
        kept, sent = add_split(kept, shifted(sent, count, third, -1), 2)
        pieces = add_split(kept, shifted(sent, count, second, -1), 4)
        received = [shifted(pieces[step], count, first, -step) for step in range(1, 4)]
        return add_all([pieces[0]] + received)
    held = jnp.concatenate([kept, sent], axis=0)
    for level in reversed(levels):
        size = level[1]
        pieces = held.reshape(size, held.shape[0] // size, held.shape[1])
        total = wide(pieces[0])
        for step in range(1, size):
            total = total + wide(shifted(pieces[step], count, level, -step))
        held = total if level == levels[0] else low(total)
    return held


def placement(count, width):
    device = lax.axis_index("dp")
    place = jnp.arange(count)
    owner, weight = jnp.zeros_like(place), 1
    for stride, size in levels_of(count):
        step = (place // weight) % size
        owner = owner + ((device // stride) % size - step + size) % size * stride
        weight *= size
    rows = width // count
    natural = (owner[:, None] * rows + jnp.arange(rows)[None, :]).reshape(width)
    return low(natural[None, :] == jnp.arange(width)[:, None])


def spec(block, *place):
    return pl.BlockSpec(block, lambda step: place)


def run(body, out_shapes, operands, specs=None, scratch=(), flops=0, limit=40):
    size = sum(a.size * a.dtype.itemsize for a in [*operands, *out_shapes])
    grid = () if specs is None else (1,)
    specs = [None] * len(operands) if specs is None else specs
    specs = [
        pl.BlockSpec(memory_space=pltpu.VMEM) if given is None else given for given in specs
    ]
    return pl.pallas_call(
        body,
        out_shape=out_shapes,
        grid=grid,
        in_specs=specs,
        out_specs=[pl.BlockSpec(memory_space=pltpu.VMEM)] * len(out_shapes),
        scratch_shapes=scratch,
        compiler_params=pltpu.CompilerParams(vmem_limit_bytes=limit * 1024 * 1024),
        cost_estimate=pl.CostEstimate(flops=flops, bytes_accessed=size, transcendentals=0),
    )(*operands)


def half(*shape):
    return jax.ShapeDtypeStruct(shape, jnp.bfloat16)


def full(*shape):
    return jax.ShapeDtypeStruct(shape, jnp.float32)


def stack_rows(pieces):
    rows, width = pieces[0].shape

    def body(*refs):
        for number, ref in enumerate(refs[:-1]):
            refs[-1][number * rows : (number + 1) * rows, :] = ref[...]

    return run(body, [half(rows * len(pieces), width)], pieces)[0]


def add_split(left, right, parts):
    rows, width = left.shape
    rows //= parts

    def body(left_ref, right_ref, *outs):
        for number, out in enumerate(outs):
            part = slice(number * rows, (number + 1) * rows)
            out[...] = low(wide(left_ref[part, :]) + wide(right_ref[part, :]))

    return run(body, [half(rows, width)] * parts, [left, right])


def add_all(pieces):
    def body(*refs):
        total = wide(refs[0][...])
        for ref in refs[1:-1]:
            total = total + wide(ref[...])
        refs[-1][...] = total

    return run(body, [full(*pieces[0].shape)], pieces)[0]


def normalize(values):
    average = jnp.mean(values, axis=-1, keepdims=True)
    centered = values - average
    variance = jnp.mean(centered * centered, axis=-1, keepdims=True)
    inverse = lax.rsqrt(variance + EPSILON)
    return centered * inverse, inverse


def norm_back(scaled, normed, inverse):
    first = jnp.mean(scaled, axis=-1, keepdims=True)
    second = jnp.mean(scaled * normed, axis=-1, keepdims=True)
    return inverse * (scaled - first - normed * second)


def partner(values):
    lane = lax.broadcasted_iota(jnp.int32, values.shape, 1)
    return jnp.where(
        lane % HD < HD // 2,
        pltpu.roll(values, LANES - HD // 2, 1),
        pltpu.roll(values, HD // 2, 1),
    )


def group(number):
    return slice(number * LANES, (number + 1) * LANES)


def rows_of(refs):
    return jnp.concatenate([ref[...] for ref in refs], axis=0)


def both_heads(values):
    lane = lax.broadcasted_iota(jnp.int32, values.shape, 1)
    nothing = jnp.zeros_like(values)
    return jnp.concatenate(
        [jnp.where(lane < HD, values, nothing), jnp.where(lane < HD, nothing, values)], axis=0
    )


def one_pair(values):
    rows = values.shape[0] // 2
    lane = lax.broadcasted_iota(jnp.int32, (rows, values.shape[1]), 1)
    return jnp.where(lane < HD, values[:rows], values[rows:])


def tiles_of(count, inner):
    for block in range(count // BLOCK):
        start = min(max(block * BLOCK - HALF, 0), count - WINDOW)
        for pair in range(inner // LANES):
            number = block * (inner // LANES) + pair
            yield number, pair, slice(block * BLOCK, (block + 1) * BLOCK), slice(start, start + WINDOW)


def prepare(tokens, cotangent, order):
    count, width = tokens.shape

    def body(tokens_ref, cotangent_ref, order_ref, inputs_ref, normed_ref, upstream_ref):
        inputs = product(tokens_ref[...], order_ref[...])
        inputs_ref[...] = low(inputs)
        normed_ref[...] = low(normalize(inputs)[0])
        upstream_ref[...] = low(product(cotangent_ref[...], order_ref[...]))

    return run(
        body, [half(count, width)] * 3, [tokens, cotangent, order], flops=4 * count * width * width
    )


def attend_shares(normed, pieces, cosine, sine, column, row):
    count, width = normed.shape
    inner = pieces[0].shape[1] // 2
    tiles = list(tiles_of(count, inner))

    def body(normed_ref, a, b, c, d, cosine_ref, sine_ref, column_ref, row_ref, query_ref, keys_ref, shares_ref):
        projected = product(normed_ref[...], rows_of((a, b, c, d)))
        cosine, sine = cosine_ref[...], sine_ref[...]
        for number in range(inner // LANES):
            part = projected[:, group(number)]
            query_ref[:, group(number)] = low(part * cosine + partner(part) * sine)
            part = projected[:, group(number + inner // LANES)]
            keys_ref[:, group(number)] = low(part * cosine + partner(part) * sine)
        for number, pair, queries, window in tiles:
            if pair == 0:
                near = lax.broadcasted_iota(jnp.int32, (WINDOW, BLOCK), 0) + window.start
                near = near - lax.broadcasted_iota(jnp.int32, (WINDOW, BLOCK), 1) - queries.start
                allowed = (jnp.abs(near) <= HALF) & (column_ref[window, :] == row_ref[:, queries])
                allowed = jnp.concatenate([allowed.astype(jnp.float32)] * 2, axis=1) > 0.5
            query = both_heads(query_ref[queries, group(pair)])
            scores = product(keys_ref[window, group(pair)], query, NT) * SCALE
            scores = jnp.where(allowed, scores, MASKED)
            powers = jnp.exp(scores - jnp.max(scores, axis=0, keepdims=True))
            total = jnp.sum(powers, axis=0, keepdims=True)
            shares_ref[number] = low(powers * (1.0 / total))

    return run(
        body,
        [half(count, inner), half(count, inner), half(len(tiles), WINDOW, 2 * BLOCK)],
        [normed, *pieces, cosine, sine, column, row],
        flops=4 * count * width * inner + len(tiles) * 4 * WINDOW * BLOCK * LANES,
    )


def attend_values(normed, pieces, shares):
    count, width = normed.shape
    inner = pieces[0].shape[1] // 2
    tiles = list(tiles_of(count, inner))
    rows = count // CHUNKS

    def body(normed_ref, a, b, c, d, shares_ref, values_ref, context_ref, *outs):
        matrix = rows_of((a, b, c, d))
        values_ref[...] = low(product(normed_ref[...], matrix[:, :inner]))
        for number, pair, queries, window in tiles:
            both = product(shares_ref[number], values_ref[window, group(pair)], TN)
            context_ref[queries, group(pair)] = low(one_pair(both))
        for number, out in enumerate(outs):
            part = context_ref[number * rows : (number + 1) * rows, :]
            out[...] = low(product(part, matrix[:, inner:], NT))

    return run(
        body,
        [half(count, inner), half(count, inner)] + [half(rows, width)] * CHUNKS,
        [normed, *pieces, shares],
        flops=4 * count * width * inner + len(tiles) * 4 * WINDOW * BLOCK * LANES,
    )


def feed_forward(number, inputs, upstream, own, other, pieces, hidden):
    count, width = inputs.shape
    rows = count // CHUNKS

    def body(inputs_ref, upstream_ref, own_ref, other_ref, a, b, c, d, e, f, g, h,
             middle_ref, normed_ref, mixed_ref, gates_ref, forward_ref, back_ref):
        middle = wide(inputs_ref[...]) + (wide(own_ref[...]) + wide(other_ref[...]))
        middle_ref[...] = middle
        normed = low(normalize(middle)[0])
        normed_ref[...] = normed
        matrix = rows_of((a, b, c, d))
        down = rows_of((e, f, g, h))
        gates = product(normed, matrix)
        active, factor = gates[:, :hidden], gates[:, hidden:]
        chance = 0.5 + 0.5 * lax.erf(active * 0.7071067811865476)
        bent = active * chance
        mixed = low(bent * factor)
        mixed_ref[...] = mixed
        forward_ref[...] = low(product(mixed, down, NT))
        grad_mixed = product(upstream_ref[...], down)
        slope = chance + active * (0.3989422804014327 * jnp.exp(-0.5 * active * active))
        grad_active = low(grad_mixed * factor * slope)
        grad_factor = low(grad_mixed * bent)
        gates_ref[:, :hidden] = grad_active
        gates_ref[:, hidden:] = grad_factor
        back_ref[...] = low(
            product(grad_active, matrix[:, :hidden], NT) + product(grad_factor, matrix[:, hidden:], NT)
        )

    chunk = spec((rows, width), number, 0)
    return run(
        body,
        [full(rows, width), half(rows, width), half(rows, hidden), half(rows, 2 * hidden), half(rows, width), half(rows, width)],
        [inputs, upstream, own, other, *pieces, *pieces],
        [chunk, chunk, None, None]
        + [spec((width // PIECES, 2 * hidden), 0, 0)] * PIECES
        + [spec((width // PIECES, hidden), 0, 2)] * PIECES,
        flops=2 * rows * width * hidden * 6,
    )


def feed_forward_grads(normed, mixed, gates, upstream):
    count, width = upstream.shape
    hidden = mixed[0].shape[1]

    def body(*refs):
        normed, mixed, gates = (rows_of(refs[i * CHUNKS : (i + 1) * CHUNKS]) for i in range(3))
        upstream = refs[3 * CHUNKS][...]
        for number, out in enumerate(refs[3 * CHUNKS + 1 :]):
            part = slice(number * width // 2, (number + 1) * width // 2)
            out[:, : 2 * hidden] = low(product(normed[:, part], gates, TN))
            out[:, 2 * hidden :] = low(product(upstream[:, part], mixed, TN))

    return run(
        body,
        [half(width // 2, 3 * hidden)] * 2,
        [*normed, *mixed, *gates, upstream],
        flops=2 * count * width * hidden * 3,
    )


def add_output(middle, own, other, order):
    rows, width = middle[0].shape

    def body(*refs):
        order = refs[3 * CHUNKS][...]
        for number in range(CHUNKS):
            middle, own, other = (refs[number + i * CHUNKS][...] for i in range(3))
            total = low(middle + (wide(own) + wide(other)))
            refs[-1][number * rows : (number + 1) * rows, :] = low(product(total, order, NT))

    return run(
        body,
        [half(rows * CHUNKS, width)],
        [*middle, *own, *other, order],
        flops=2 * rows * CHUNKS * width * width,
    )[0]


def attend_back_values(upstream, middle, own, other, pieces, context, shares):
    count, width = upstream.shape
    inner = context.shape[1]
    tiles = list(tiles_of(count, inner))
    rows = count // CHUNKS

    def body(upstream_ref, *refs):
        middle, own, other = (refs[i * CHUNKS : (i + 1) * CHUNKS] for i in range(3))
        refs = refs[3 * CHUNKS :]
        matrix = rows_of(refs[:PIECES])
        context_ref, shares_ref, grad_middle_ref, branch_ref, grad_context_ref, grad_values_ref, total_ref = refs[PIECES:]
        for number in range(CHUNKS):
            part = slice(number * rows, (number + 1) * rows)
            normed, inverse = normalize(middle[number][...])
            scaled = wide(own[number][...]) + wide(other[number][...])
            grad_middle = wide(upstream_ref[part, :]) + norm_back(scaled, normed, inverse)
            grad_middle_ref[part, :] = grad_middle
            branch_ref[part, :] = low(grad_middle)
        grad_context_ref[...] = low(product(branch_ref[...], matrix))
        total_ref[...] = jnp.zeros_like(total_ref)
        for number, pair, queries, window in tiles:
            upper = both_heads(grad_context_ref[queries, group(pair)])
            total_ref[window, group(pair)] += product(shares_ref[number], upper)
        grad_values_ref[...] = low(total_ref[...])

    return run(
        body,
        [full(count, width), half(count, width), half(count, inner), half(count, inner)],
        [upstream, *middle, *own, *other, *pieces, context, shares],
        [None] * (1 + 3 * CHUNKS) + [spec((width // PIECES, inner), 0, 1)] * PIECES + [None] * 2,
        scratch=[pltpu.VMEM((count, inner), jnp.float32)],
        flops=2 * count * width * inner + len(tiles) * 4 * WINDOW * BLOCK * LANES,
    )


def attend_back_shares(query, keys, values, grad_context, shares, grad_values, cosine, sine, query_keys, values_out):
    count, inner = query.shape
    width = query_keys[0].shape[0] * PIECES
    tiles = list(tiles_of(count, inner))

    def body(query_ref, keys_ref, values_ref, grad_context_ref, shares_ref, grad_values_ref, cosine_ref, sine_ref,
             a, b, c, d, e, f, g, h, grad_ref, back_ref, total_ref):
        total_ref[...] = jnp.zeros_like(total_ref)
        cosine, sine = cosine_ref[...], sine_ref[...]
        for number, pair, queries, window in tiles:
            upper = both_heads(grad_context_ref[queries, group(pair)])
            grad_shares = product(values_ref[window, group(pair)], upper, NT)
            shares = wide(shares_ref[number])
            sums = jnp.sum(shares * grad_shares, axis=0, keepdims=True)
            grad_scores = low(shares * (grad_shares - sums))
            grad_query = one_pair(product(grad_scores, keys_ref[window, group(pair)], TN)) * SCALE
            grad_query = grad_query * cosine[queries] - partner(grad_query) * sine[queries]
            grad_ref[queries, group(pair)] = low(grad_query)
            lower = both_heads(query_ref[queries, group(pair)])
            total_ref[window, group(pair)] += product(grad_scores, lower)
        for pair in range(inner // LANES):
            grad_keys = total_ref[:, group(pair)] * SCALE
            grad_keys = grad_keys * cosine - partner(grad_keys) * sine
            grad_ref[:, group(pair + inner // LANES)] = low(grad_keys)
        back = product(grad_ref[...], rows_of((a, b, c, d)), NT)
        back_ref[...] = low(back + product(grad_values_ref[...], rows_of((e, f, g, h)), NT))

    return run(
        body,
        [half(count, 2 * inner), half(count, width)],
        [query, keys, values, grad_context, shares, grad_values, cosine, sine, *query_keys, *values_out],
        [None] * (8 + PIECES) + [spec((width // PIECES, inner), 0, 0)] * PIECES,
        scratch=[pltpu.VMEM((count, inner), jnp.float32)],
        flops=6 * count * width * inner + len(tiles) * 12 * WINDOW * BLOCK * LANES,
    )


def paired_grads(pairs):
    count, width = pairs[0][0].shape
    sizes = [right.shape[1] for _, right in pairs]

    def body(*refs):
        outs = refs[2 * len(pairs) :]
        for number, out in enumerate(outs):
            part = slice(number * width // 2, (number + 1) * width // 2)
            start = 0
            for i, size in enumerate(sizes):
                out[:, start : start + size] = low(product(refs[2 * i][:, part], refs[2 * i + 1][...], TN))
                start += size

    return run(
        body,
        [half(width // 2, sum(sizes))] * 2,
        [array for pair in pairs for array in pair],
        flops=2 * count * width * sum(sizes),
    )


def input_grads(grad_middle, inputs, own, other, order):
    count, width = inputs.shape

    def body(grad_middle_ref, inputs_ref, own_ref, other_ref, order_ref, out_ref):
        normed, inverse = normalize(wide(inputs_ref[...]))
        scaled = wide(own_ref[...]) + wide(other_ref[...])
        total = grad_middle_ref[...] + norm_back(scaled, normed, inverse)
        high = low(total)
        rest = low(total - wide(high))
        out_ref[...] = product(high, order_ref[...], NT) + product(rest, order_ref[...], NT)

    return run(
        body,
        [full(count, width)],
        [grad_middle, inputs, own, other, order],
        flops=4 * count * width * width,
    )[0]


def rope_tables(positions):
    frequency = THETA ** (-jnp.arange(0, HD, 2).astype(jnp.float32) / HD)
    angle = positions.astype(jnp.float32)[:, None] * jnp.tile(frequency, LANES // (HD // 2))[None, :]
    sign = jnp.where(jnp.arange(LANES) % HD < HD // 2, -1.0, 1.0)
    return jnp.cos(angle), jnp.sin(angle) * sign[None, :]


def padded(values, width):
    return jnp.pad(values, ((0, 0), (0, width - values.shape[1])))


def per_device(
    devices, tokens, seg_ids, positions, gain_attn, w_qkv, w_attn_out, gain_mlp, w_in, w_mlp_out, cotangent
):
    width = tokens.shape[1]
    rows, _, inner = w_qkv.shape
    hidden = w_in.shape[2]
    room = -(-hidden // LANES) * LANES
    gain_one, gain_two = wide(gain_attn)[:, None], wide(gain_mlp)[:, None]
    scaled_qkv = [low(wide(w_qkv[:, i]) * gain_one) for i in range(3)]
    scaled_in = [padded(low(wide(w_in[:, i]) * gain_two), room) for i in range(2)]
    shard_one = jnp.concatenate(scaled_qkv[:2], axis=1)
    shard_two = jnp.concatenate([scaled_qkv[2], w_attn_out.T], axis=1)
    shard_three = jnp.concatenate(scaled_in + [padded(w_mlp_out.T, room)], axis=1)
    query_keys = gather_rows(shard_one, devices)
    values_out = gather_rows(shard_two, devices)
    shard_three, _ = lax.optimization_barrier((shard_three, values_out[0]))
    gates_down = gather_rows(shard_three, devices)

    order = placement(devices, width)
    inputs, normed_one, upstream = prepare(tokens, cotangent, order)
    cosine, sine = rope_tables(positions)
    query, keys, shares = attend_shares(
        normed_one, query_keys, cosine, sine, seg_ids[:, None], seg_ids[None, :]
    )
    values, context, *own = attend_values(normed_one, values_out, shares)
    other = [swapped(part) for part in own]
    middle, normed_two, mixed, grad_gates, own_out, own_two = zip(
        *(
            feed_forward(number, inputs, upstream, own[number], other[number], gates_down, room)
            for number in range(CHUNKS)
        )
    )
    other_two = [swapped(part) for part in own_two]
    other_out = [swapped(part) for part in own_out]
    grads_mlp = feed_forward_grads(normed_two, mixed, grad_gates, upstream)
    grads_mlp = scatter_rows(*grads_mlp, devices, rows)
    output = add_output(middle, own_out, other_out, order)
    grad_middle, branch, grad_context, grad_values = attend_back_values(
        upstream, middle, own_two, other_two, values_out, context, shares
    )
    grads_two = scatter_rows(
        *paired_grads([(normed_one, grad_values), (branch, context)]), devices, rows
    )
    grad_query_keys, own_one = attend_back_shares(
        query, keys, values, grad_context, shares, grad_values, cosine, sine, query_keys, values_out
    )
    other_one = swapped(own_one)
    grads_one = scatter_rows(*paired_grads([(normed_one, grad_query_keys)]), devices, rows)
    grad_input = input_grads(grad_middle, inputs, own_one, other_one, order)

    sum_qkv = [grads_one[:, :inner], grads_one[:, inner:], grads_two[:, :inner]]
    sum_in = [grads_mlp[:, :hidden], grads_mlp[:, room : room + hidden]]
    gains = jnp.stack(
        [
            sum(jnp.sum(wide(w_qkv[:, i]) * part, axis=1) for i, part in enumerate(sum_qkv)),
            sum(jnp.sum(wide(w_in[:, i]) * part, axis=1) for i, part in enumerate(sum_in)),
        ]
    )
    gains = gains + swapped(gains)
    return (
        output,
        grad_input,
        gains[0],
        jnp.stack([part * gain_one for part in sum_qkv], axis=1),
        grads_two[:, inner:].T,
        gains[1],
        jnp.stack([part * gain_two for part in sum_in], axis=1),
        grads_mlp[:, 2 * room : 2 * room + hidden].T,
    )


def solution(mesh):
    return jax.shard_map(
        functools.partial(per_device, mesh.shape["dp"]),
        mesh=mesh,
        in_specs=(
            P("dp", None),
            P("dp"),
            P("dp"),
            P("dp"),
            P("dp", None, "tensor"),
            P("tensor", "dp"),
            P("dp"),
            P("dp", None, "tensor"),
            P("tensor", "dp"),
            P("dp", None),
        ),
        out_specs=(
            P("dp", None),
            P("dp", None),
            P("dp"),
            P("dp", None, "tensor"),
            P("tensor", "dp"),
            P("dp"),
            P("dp", None, "tensor"),
            P("tensor", "dp"),
        ),
        check_vma=False,
    )
```

```python
import functools

import jax
import jax.numpy as jnp
from jax import lax
from jax.experimental import pallas as pl
from jax.experimental.pallas import tpu as pltpu
from jax.sharding import PartitionSpec as P

HD = 64
HALF = 64
LIMIT = 16
SMALL = 4
LANES = 128
BLOCK = 128
WINDOW = 256
PIECES = 4

EPSILON = 1e-05
THETA = 10000.0
MASKED = -1e30
SCALE = HD ** (-0.5)

NN = (((1,), (0,)), ((), ()))
NT = (((1,), (1,)), ((), ()))
TN = (((0,), (0,)), ((), ()))


def product(left, right, dims=NN):
    return lax.dot_general(left, right, dims, preferred_element_type=jnp.float32)


def low(values):
    return values.astype(jnp.bfloat16)


def wide(values):
    return values.astype(jnp.float32)


def levels_of(count):
    levels, stride = [], count
    while stride > 1:
        size = 4 if stride % 8 == 0 else 2 if stride % 2 == 0 else stride
        stride //= size
        levels.append((stride, size))
    return levels


def shifted(values, count, level, step):
    stride, size = level
    pairs = []
    for device in range(count):
        digit = (device // stride) % size
        pairs.append((device, device + ((digit + step) % size - digit) * stride))
    return lax.ppermute(values, "dp", pairs)


def swapped(values):
    return lax.ppermute(values, "tensor", [(0, 1), (1, 0)])


def is_plain(count, rows):
    return levels_of(count) == [(4, 4), (2, 2), (1, 2)] and rows % 16 == 0


def after(values, *others):
    return lax.optimization_barrier((values, *others))[0]


class Gather:
    def __init__(self, shard, count, late=False, tail=False):
        self.count, self.levels, self.late, self.tail = count, levels_of(count), late, tail
        self.plain = is_plain(count, shard.shape[0])
        self.shard = shard
        if not self.plain:
            held = shard
            for level in self.levels:
                held = jnp.concatenate(
                    [held] + [shifted(held, count, level, step) for step in range(1, level[1])], axis=0
                )
            self.pieces = jnp.split(held, PIECES, axis=0)
            self.other = self.pieces[0]
        elif late:
            self.other = shifted(shard, count, self.levels[1], 1)
        else:
            self.received = self.along_first(shard)

    def along_first(self, rows):
        return [shifted(rows, self.count, self.levels[0], step) for step in range(1, 4)]

    def join_rows(self):
        if self.plain:
            self.shard = stack_rows([self.shard, self.other])

    def begin(self, other):
        if self.plain:
            self.shard = after(self.shard, other)
            self.received = self.along_first(self.shard)

    def stack(self):
        if self.plain:
            _, second, third = self.levels
            if self.late:
                held, other = stack_rows([self.shard] + self.received, 2)
            else:
                held = stack_rows([self.shard] + self.received)
                other = self.other = shifted(held, self.count, second, 1)
            self.pieces = [held, other]
            if not self.tail:
                self.share()
        return self.pieces[0]

    def share(self, *others):
        if self.plain:
            self.pieces += [
                shifted(after(part, *others), self.count, self.levels[2], 1) for part in self.pieces
            ]


class Scatter:
    def __init__(self, kept, sent, count, rows):
        self.count, self.levels = count, levels_of(count)
        self.plain = is_plain(count, rows)
        if self.plain:
            self.own, self.other = kept, [shifted(part, count, self.levels[2], -1) for part in sent]
            return
        held = jnp.concatenate([jnp.concatenate(side, axis=1) for side in (kept, sent)], axis=0)
        for level in reversed(self.levels):
            size = level[1]
            pieces = held.reshape(size, held.shape[0] // size, held.shape[1])
            total = wide(pieces[0])
            for step in range(1, size):
                total = total + wide(shifted(pieces[step], count, level, -step))
            held = total if level == self.levels[0] else low(total)
        self.other = self.begun = held
        self.parts = [held]

    def second(self, *others):
        if self.plain:
            self.own, sent = add_split(self.own, self.other, 2)
            self.other = shifted(after(sent, *others), self.count, self.levels[1], -1)

    def third(self):
        if self.plain:
            pieces = add_split([self.own], [self.other], 4)
            self.parts = [pieces[0]]
            for step in range(1, 4):
                self.parts.append(shifted(pieces[step], self.count, self.levels[0], -step))
            self.other, self.begun = self.parts[1:], pieces[0]

def placement(count, width):
    device = lax.axis_index("dp")
    place = jnp.arange(count)
    owner, weight = jnp.zeros_like(place), 1
    for stride, size in levels_of(count):
        step = (place // weight) % size
        owner = owner + ((device // stride) % size - step + size) % size * stride
        weight *= size
    rows = width // count
    natural = (owner[:, None] * rows + jnp.arange(rows)[None, :]).reshape(width)
    return low(natural[None, :] == jnp.arange(width)[:, None])


def spec(block, *place):
    return pl.BlockSpec(block, lambda step: place)


latest = []


def wait_for(*arrays):
    latest.extend(arrays)


def run(body, out_shapes, operands, specs=None, scratch=(), limit=LIMIT, last=False):
    if last:
        limit = 60
        specs = [spec(array.shape, *[0] * array.ndim) for array in operands]
    grid = () if specs is None else (1,)
    specs = [None] * len(operands) if specs is None else specs
    specs = [
        pl.BlockSpec(memory_space=pltpu.VMEM) if given is None else given for given in specs
    ]
    count, waits = len(operands), len(latest)

    def ordered(*refs):
        body(*refs[:count], *refs[count + waits :])

    results = pl.pallas_call(
        ordered,
        out_shape=out_shapes,
        grid=grid,
        in_specs=specs + [pl.BlockSpec(memory_space=pl.ANY)] * waits,
        out_specs=[
            spec(shape.shape, *[0] * len(shape.shape)) if last else pl.BlockSpec(memory_space=pltpu.VMEM)
            for shape in out_shapes
        ],
        scratch_shapes=scratch,
        compiler_params=pltpu.CompilerParams(vmem_limit_bytes=limit * 1024 * 1024),
        cost_estimate=pl.CostEstimate(flops=0, bytes_accessed=0, transcendentals=0),
    )(*operands, *latest)
    latest[:] = [min(results, key=lambda array: array.size)]
    return results


def half(*shape):
    return jax.ShapeDtypeStruct(shape, jnp.bfloat16)


def full(*shape):
    return jax.ShapeDtypeStruct(shape, jnp.float32)


def stack_rows(pieces, parts=1):
    rows, width = pieces[0].shape
    rows //= parts

    def body(*refs):
        for number, ref in enumerate(refs[:-parts]):
            for part, out in enumerate(refs[-parts:]):
                out[number * rows : (number + 1) * rows, :] = ref[part * rows : (part + 1) * rows, :]

    stacked = run(body, [half(rows * len(pieces), width)] * parts, pieces, limit=SMALL)
    return stacked if parts > 1 else stacked[0]


def add_split(left, right, parts):
    rows = left[0].shape[0] // parts
    sizes = [piece.shape[1] for piece in left]

    def body(*refs):
        start = 0
        for i, size in enumerate(sizes):
            for number, out in enumerate(refs[2 * len(sizes) :]):
                part = slice(number * rows, (number + 1) * rows)
                total = wide(refs[i][part, :]) + wide(refs[i + len(sizes)][part, :])
                out[:, start : start + size] = low(total)
            start += size

    return run(body, [half(rows, sum(sizes))] * parts, [*left, *right], limit=SMALL)


def total_of(refs):
    total = wide(refs[0][...])
    for ref in refs[1:]:
        total = total + wide(ref[...])
    return total


def add_all(parts):
    def body(*refs):
        refs[-1][...] = total_of(refs[:-1])

    return run(body, [full(*parts[0].shape)], parts, limit=SMALL)[0]


def finish_feed_forward(active, others, weights, gain, hidden):
    rows, room = active.shape

    def body(active_ref, others_ref, weights_ref, gain_ref, sum_ref, down_ref, share_ref):
        active, factor = active_ref[...], others_ref[:, :room]
        down_ref[...] = others_ref[:, room : room + hidden]
        sum_ref[:, 0, :] = active[:, :hidden] * gain_ref[...]
        sum_ref[:, 1, :] = factor[:, :hidden] * gain_ref[...]
        share = wide(weights_ref[:, :room]) * active + wide(weights_ref[:, room:]) * factor
        share_ref[...] = jnp.sum(share, axis=1, keepdims=True) / gain_ref[...]

    return run(
        body,
        [full(rows, 2, hidden), full(rows, hidden), full(rows, 1)],
        [active, others, weights, gain],
        last=True,
    )


def finish_attention(parts, query_keys, values_out, gain, share):
    rows, inner = values_out.shape[0], values_out.shape[1] // 2

    def body(*refs):
        *parts, query_keys_ref, values_out_ref, gain_ref, other_ref, sum_ref, out_ref, share_ref = refs
        total = total_of(parts)
        for number in range(3):
            sum_ref[:, number, :] = total[:, number * inner : (number + 1) * inner] * gain_ref[...]
        out_ref[...] = total[:, 3 * inner :]
        share = jnp.sum(wide(query_keys_ref[...]) * total[:, : 2 * inner], axis=1, keepdims=True)
        values = wide(values_out_ref[:, :inner]) * total[:, 2 * inner : 3 * inner]
        share = (share + jnp.sum(values, axis=1, keepdims=True)) / gain_ref[...]
        lane = lax.broadcasted_iota(jnp.int32, (rows, 2), 1)
        share_ref[...] = jnp.where(lane == 0, share, other_ref[...])

    return run(
        body,
        [full(rows, 3, inner), full(rows, inner), full(rows, 2)],
        [*parts, query_keys, values_out, gain, share],
        last=True,
    )


def normalize(values):
    average = jnp.mean(values, axis=-1, keepdims=True)
    centered = values - average
    variance = jnp.mean(centered * centered, axis=-1, keepdims=True)
    inverse = lax.rsqrt(variance + EPSILON)
    return centered * inverse, inverse


def norm_back(scaled, normed, inverse):
    first = jnp.mean(scaled, axis=-1, keepdims=True)
    second = jnp.mean(scaled * normed, axis=-1, keepdims=True)
    return inverse * (scaled - first - normed * second)


def partner(values):
    lane = lax.broadcasted_iota(jnp.int32, values.shape, 1)
    return jnp.where(
        lane % HD < HD // 2,
        pltpu.roll(values, LANES - HD // 2, 1),
        pltpu.roll(values, HD // 2, 1),
    )


def group(number):
    return slice(number * LANES, (number + 1) * LANES)


def rows_of(refs):
    return jnp.concatenate([ref[...] for ref in refs], axis=0)


def both_heads(values):
    lane = lax.broadcasted_iota(jnp.int32, values.shape, 1)
    nothing = jnp.zeros_like(values)
    return jnp.concatenate(
        [jnp.where(lane < HD, values, nothing), jnp.where(lane < HD, nothing, values)], axis=0
    )


def one_pair(values):
    rows = values.shape[0] // 2
    lane = lax.broadcasted_iota(jnp.int32, (rows, values.shape[1]), 1)
    return jnp.where(lane < HD, values[:rows], values[rows:])


def tiles_of(count, inner):
    for block in range(count // BLOCK):
        start = min(max(block * BLOCK - HALF, 0), count - WINDOW)
        for pair in range(inner // LANES):
            number = block * (inner // LANES) + pair
            yield number, pair, slice(block * BLOCK, (block + 1) * BLOCK), slice(start, start + WINDOW)


def prepare(tokens, cotangent, order):
    count, width = tokens.shape

    def body(tokens_ref, cotangent_ref, order_ref, inputs_ref, normed_ref, upstream_ref):
        inputs = product(tokens_ref[...], order_ref[...])
        inputs_ref[...] = low(inputs)
        normed_ref[...] = low(normalize(inputs)[0])
        upstream_ref[...] = low(product(cotangent_ref[...], order_ref[...]))

    return run(
        body, [half(count, width)] * 3, [tokens, cotangent, order]
    )


def attend_shares(normed, pieces, cosine, sine, column, row):
    count, width = normed.shape
    inner = pieces[0].shape[1] // 2
    tiles = list(tiles_of(count, inner))

    def body(normed_ref, a, b, c, d, cosine_ref, sine_ref, column_ref, row_ref, query_ref, keys_ref, shares_ref):
        projected = product(normed_ref[...], rows_of((a, b, c, d)))
        cosine, sine = cosine_ref[...], sine_ref[...]
        for number in range(inner // LANES):
            part = projected[:, group(number)]
            query_ref[:, group(number)] = low(part * cosine + partner(part) * sine)
            part = projected[:, group(number + inner // LANES)]
            keys_ref[:, group(number)] = low(part * cosine + partner(part) * sine)
        for number, pair, queries, window in tiles:
            if pair == 0:
                near = lax.broadcasted_iota(jnp.int32, (WINDOW, BLOCK), 0) + window.start
                near = near - lax.broadcasted_iota(jnp.int32, (WINDOW, BLOCK), 1) - queries.start
                allowed = (jnp.abs(near) <= HALF) & (column_ref[window, :] == row_ref[:, queries])
                allowed = jnp.concatenate([allowed.astype(jnp.float32)] * 2, axis=1) > 0.5
            query = both_heads(query_ref[queries, group(pair)])
            scores = product(keys_ref[window, group(pair)], query, NT) * SCALE
            scores = jnp.where(allowed, scores, MASKED)
            powers = jnp.exp(scores - jnp.max(scores, axis=0, keepdims=True))
            total = jnp.sum(powers, axis=0, keepdims=True)
            shares_ref[number] = low(powers * (1.0 / total))

    return run(
        body,
        [half(count, inner), half(count, inner), half(len(tiles), WINDOW, 2 * BLOCK)],
        [normed, *pieces, cosine, sine, column, row],
    )


def attend_values(normed, pieces, shares):
    count, width = normed.shape
    inner = pieces[0].shape[1] // 2
    tiles = list(tiles_of(count, inner))

    def body(normed_ref, a, b, c, d, shares_ref, values_ref, context_ref, out_ref):
        matrix = rows_of((a, b, c, d))
        values_ref[...] = low(product(normed_ref[...], matrix[:, :inner]))
        for number, pair, queries, window in tiles:
            both = product(shares_ref[number], values_ref[window, group(pair)], TN)
            context_ref[queries, group(pair)] = low(one_pair(both))
        out_ref[...] = low(product(context_ref[...], matrix[:, inner:], NT))

    return run(
        body,
        [half(count, inner), half(count, inner), half(count, width)],
        [normed, *pieces, shares],
    )


def feed_forward(inputs, upstream, own, other, gates_in, down):
    count, width = inputs.shape
    hidden = down[0].shape[1]

    def body(inputs_ref, upstream_ref, own_ref, other_ref, a, b, c, d, e, f, g, h,
             middle_ref, normed_ref, mixed_ref, gates_ref, forward_ref, back_ref):
        middle = wide(inputs_ref[...]) + (wide(own_ref[...]) + wide(other_ref[...]))
        middle_ref[...] = middle
        normed = low(normalize(middle)[0])
        normed_ref[...] = normed
        matrix, down = rows_of((a, b, c, d)), rows_of((e, f, g, h))
        gates = product(normed, matrix)
        active, factor = gates[:, :hidden], gates[:, hidden:]
        chance = 0.5 + 0.5 * lax.erf(active * 0.7071067811865476)
        bent = active * chance
        mixed = low(bent * factor)
        mixed_ref[...] = mixed
        forward_ref[...] = low(product(mixed, down, NT))
        grad_mixed = product(upstream_ref[...], down)
        slope = chance + active * (0.3989422804014327 * jnp.exp(-0.5 * active * active))
        gates_ref[:, :hidden] = low(grad_mixed * factor * slope)
        gates_ref[:, hidden:] = low(grad_mixed * bent)
        back_ref[...] = low(product(gates_ref[...], matrix, NT))

    return run(
        body,
        [full(count, width), half(count, width), half(count, hidden), half(count, 2 * hidden)]
        + [half(count, width)] * 2,
        [inputs, upstream, own, other, *gates_in, *down],
    )


def feed_forward_grads(normed, mixed, gates, upstream):
    count, width = upstream.shape
    hidden = mixed.shape[1]

    def body(normed_ref, mixed_ref, gates_ref, upstream_ref, *outs):
        for number in range(2):
            part = slice(number * width // 2, (number + 1) * width // 2)
            active_ref, factor_ref, down_ref = outs[3 * number : 3 * number + 3]
            both = product(normed_ref[:, part], gates_ref[...], TN)
            active_ref[...] = low(both[:, :hidden])
            factor_ref[...] = low(both[:, hidden:])
            down_ref[...] = low(product(upstream_ref[:, part], mixed_ref[...], TN))

    return run(body, [half(width // 2, hidden)] * 6, [normed, mixed, gates, upstream])


def add_output(middle, own, other, order):
    def body(middle_ref, own_ref, other_ref, order_ref, out_ref):
        total = low(middle_ref[...] + (wide(own_ref[...]) + wide(other_ref[...])))
        out_ref[...] = low(product(total, order_ref[...], NT))

    return run(body, [half(*middle.shape)], [middle, own, other, order], last=True)[0]


def attend_back_values(upstream, middle, own, other, pieces, context, shares):
    count, width = upstream.shape
    inner = context.shape[1]
    tiles = list(tiles_of(count, inner))

    def body(upstream_ref, middle_ref, own_ref, other_ref, a, b, c, d, context_ref, shares_ref,
             grad_middle_ref, branch_ref, grad_context_ref, grad_values_ref, total_ref):
        matrix = rows_of((a, b, c, d))
        normed, inverse = normalize(middle_ref[...])
        scaled = wide(own_ref[...]) + wide(other_ref[...])
        grad_middle = wide(upstream_ref[...]) + norm_back(scaled, normed, inverse)
        grad_middle_ref[...] = grad_middle
        branch_ref[...] = low(grad_middle)
        grad_context_ref[...] = low(product(branch_ref[...], matrix))
        total_ref[...] = jnp.zeros_like(total_ref)
        for number, pair, queries, window in tiles:
            upper = both_heads(grad_context_ref[queries, group(pair)])
            total_ref[window, group(pair)] += product(shares_ref[number], upper)
        grad_values_ref[...] = low(total_ref[...])

    return run(
        body,
        [full(count, width), half(count, width), half(count, inner), half(count, inner)],
        [upstream, middle, own, other, *pieces, context, shares],
        [None] * 4 + [spec((width // PIECES, inner), 0, 1)] * PIECES + [None] * 2,
        scratch=[pltpu.VMEM((count, inner), jnp.float32)],
    )


def attend_back_shares(query, keys, values, grad_context, shares, grad_values, cosine, sine, query_keys, values_out):
    count, inner = query.shape
    width = query_keys[0].shape[0] * PIECES
    tiles = list(tiles_of(count, inner))

    def body(query_ref, keys_ref, values_ref, grad_context_ref, shares_ref, grad_values_ref, cosine_ref, sine_ref,
             a, b, c, d, e, f, g, h, grad_ref, back_ref, total_ref):
        total_ref[...] = jnp.zeros_like(total_ref)
        cosine, sine = cosine_ref[...], sine_ref[...]
        for number, pair, queries, window in tiles:
            upper = both_heads(grad_context_ref[queries, group(pair)])
            grad_shares = product(values_ref[window, group(pair)], upper, NT)
            shares = wide(shares_ref[number])
            sums = jnp.sum(shares * grad_shares, axis=0, keepdims=True)
            grad_scores = low(shares * (grad_shares - sums))
            grad_query = one_pair(product(grad_scores, keys_ref[window, group(pair)], TN)) * SCALE
            grad_query = grad_query * cosine[queries] - partner(grad_query) * sine[queries]
            grad_ref[queries, group(pair)] = low(grad_query)
            lower = both_heads(query_ref[queries, group(pair)])
            total_ref[window, group(pair)] += product(grad_scores, lower)
        for pair in range(inner // LANES):
            grad_keys = total_ref[:, group(pair)] * SCALE
            grad_keys = grad_keys * cosine - partner(grad_keys) * sine
            grad_ref[:, group(pair + inner // LANES)] = low(grad_keys)
        back = product(grad_ref[...], rows_of((a, b, c, d)), NT)
        back_ref[...] = low(back + product(grad_values_ref[...], rows_of((e, f, g, h)), NT))

    return run(
        body,
        [half(count, 2 * inner), half(count, width)],
        [query, keys, values, grad_context, shares, grad_values, cosine, sine, *query_keys, *values_out],
        [None] * (8 + PIECES) + [spec((width // PIECES, inner), 0, 0)] * PIECES,
        scratch=[pltpu.VMEM((count, inner), jnp.float32)],
    )


def paired_grads(groups):
    pairs = [pair for group in groups for pair in group]
    count, width = pairs[0][0].shape
    sizes = [sum(right.shape[1] for _, right in group) for group in groups]

    def body(*refs):
        outs, number = refs[2 * len(pairs) :], 0
        for i, group in enumerate(groups):
            start = 0
            for _, right in group:
                size = right.shape[1]
                for side in range(2):
                    part = slice(side * width // 2, (side + 1) * width // 2)
                    both = product(refs[2 * number][:, part], refs[2 * number + 1][...], TN)
                    outs[2 * i + side][:, start : start + size] = low(both)
                start += size
                number += 1

    return run(
        body,
        [half(width // 2, size) for size in sizes for _ in range(2)],
        [array for pair in pairs for array in pair],
    )


def input_grads(grad_middle, inputs, own, other, order):
    count, width = inputs.shape

    def body(grad_middle_ref, inputs_ref, own_ref, other_ref, order_ref, out_ref):
        normed, inverse = normalize(wide(inputs_ref[...]))
        scaled = wide(own_ref[...]) + wide(other_ref[...])
        total = grad_middle_ref[...] + norm_back(scaled, normed, inverse)
        high = low(total)
        rest = low(total - wide(high))
        out_ref[...] = product(high, order_ref[...], NT) + product(rest, order_ref[...], NT)

    return run(
        body,
        [full(count, width)],
        [grad_middle, inputs, own, other, order],
        last=True,
    )[0]


def rope_tables(positions):
    frequency = THETA ** (-jnp.arange(0, HD, 2).astype(jnp.float32) / HD)
    angle = positions.astype(jnp.float32)[:, None] * jnp.tile(frequency, LANES // (HD // 2))[None, :]
    sign = jnp.where(jnp.arange(LANES) % HD < HD // 2, -1.0, 1.0)
    return jnp.cos(angle), jnp.sin(angle) * sign[None, :]


def padded(values, width):
    return jnp.pad(values, ((0, 0), (0, width - values.shape[1])))


def per_device(
    devices, tokens, seg_ids, positions, gain_attn, w_qkv, w_attn_out, gain_mlp, w_in, w_mlp_out, cotangent
):
    width = tokens.shape[1]
    rows, _, inner = w_qkv.shape
    hidden = w_in.shape[2]
    room = -(-hidden // LANES) * LANES
    gain_one, gain_two = wide(gain_attn)[:, None], wide(gain_mlp)[:, None]
    scaled_qkv = [low(wide(w_qkv[:, i]) * gain_one) for i in range(3)]
    scaled_in = [padded(low(wide(w_in[:, i]) * gain_two), room) for i in range(2)]
    shard_one = jnp.concatenate(scaled_qkv[:2], axis=1)
    shard_two = jnp.concatenate([scaled_qkv[2], w_attn_out.T], axis=1)
    shard_three = jnp.concatenate(scaled_in, axis=1)
    shard_four = padded(w_mlp_out.T, room)
    latest.clear()
    query_keys = Gather(shard_one, devices)
    down = Gather(shard_four, devices, late=True)
    order = placement(devices, width)
    cosine, sine = rope_tables(positions)
    column, row = seg_ids[:, None], seg_ids[None, :]
    wait_for(cosine, sine, column)
    inputs, normed_one, upstream = prepare(tokens, cotangent, order)
    down.join_rows()
    held = query_keys.stack()
    values_out = Gather(after(shard_two, held), devices)
    wait_for(query_keys.other)
    held = values_out.stack()
    gates_in = Gather(after(shard_three, held), devices, tail=True)
    query, keys, shares = attend_shares(normed_one, query_keys.pieces, cosine, sine, column, row)
    values, context, own = attend_values(normed_one, values_out.pieces, shares)
    other = swapped(own)
    wait_for(values_out.other)
    held = gates_in.stack()
    down.begin(held)
    wait_for(other)
    gates_in.share(down.stack())
    middle, normed_two, mixed, grad_gates, own_out, own_two = feed_forward(
        inputs, upstream, own, other, gates_in.pieces, down.pieces
    )
    other_two = swapped(own_two)
    grads_mlp = feed_forward_grads(normed_two, mixed, grad_gates, upstream)
    sums_active = Scatter(grads_mlp[:1], grads_mlp[3:4], devices, rows)
    sums_others = Scatter(grads_mlp[1:3], grads_mlp[4:], devices, rows)
    sums_active.second()
    sums_others.second(sums_active.other)
    sums_active.third()
    grad_middle, branch, grad_context, grad_values = attend_back_values(
        upstream, middle, own_two, other_two, values_out.pieces, context, shares
    )
    grad_query_keys, own_one = attend_back_shares(
        query, keys, values, grad_context, shares, grad_values, cosine, sine, query_keys.pieces, values_out.pieces
    )
    other_one = swapped(own_one)
    sum_active = add_all(sums_active.parts)
    wait_for(sums_others.other)
    kept, sent = paired_grads(
        [[(normed_one, grad_query_keys), (normed_one, grad_values), (branch, context)]]
    )
    sums = Scatter([kept], [sent], devices, rows)
    sums_others.third()
    sums.second()
    sum_others = add_all(sums_others.parts)
    wait_for(other_one)
    sums.third()
    other_out = swapped(after(own_out, sums.begun))
    sum_in, sum_down, share = finish_feed_forward(
        sum_active, sum_others, shard_three, gain_two, hidden
    )
    grad_input = input_grads(grad_middle, inputs, own_one, other_one, order)
    sum_qkv, sum_out, share = finish_attention(sums.parts, shard_one, shard_two, gain_one, share)
    output = add_output(middle, own_out, other_out, order)
    gains = after(share, output) + swapped(share)
    return (output, grad_input, gains[:, 0], sum_qkv, sum_out.T, gains[:, 1], sum_in, sum_down.T)


def solution(mesh):
    return jax.shard_map(
        functools.partial(per_device, mesh.shape["dp"]),
        mesh=mesh,
        in_specs=(
            P("dp", None),
            P("dp"),
            P("dp"),
            P("dp"),
            P("dp", None, "tensor"),
            P("tensor", "dp"),
            P("dp"),
            P("dp", None, "tensor"),
            P("tensor", "dp"),
            P("dp", None),
        ),
        out_specs=(
            P("dp", None),
            P("dp", None),
            P("dp"),
            P("dp", None, "tensor"),
            P("tensor", "dp"),
            P("dp"),
            P("dp", None, "tensor"),
            P("tensor", "dp"),
        ),
        check_vma=False,
    )
```

```python
import functools

import jax
import jax.numpy as jnp
from jax import lax
from jax.experimental import pallas as pl
from jax.experimental.pallas import tpu as pltpu
from jax.sharding import PartitionSpec as P

HD = 64
HALF = 64
LIMIT = 16
SMALL = 4
LANES = 128
BLOCK = 128
WINDOW = 256
EARLY = 4
WEIGHT = 10**10
PIECES = 4

EPSILON = 1e-05
THETA = 10000.0
MASKED = -1e30
SCALE = HD ** (-0.5)

NN = (((1,), (0,)), ((), ()))
NT = (((1,), (1,)), ((), ()))
TN = (((0,), (0,)), ((), ()))


def product(left, right, dims=NN):
    return lax.dot_general(left, right, dims, preferred_element_type=jnp.float32)


def low(values):
    return values.astype(jnp.bfloat16)


def wide(values):
    return values.astype(jnp.float32)


def levels_of(count):
    levels, stride = [], count
    while stride > 1:
        size = 4 if stride % 8 == 0 else 2 if stride % 2 == 0 else stride
        stride //= size
        levels.append((stride, size))
    return levels


def shifted(values, count, level, step):
    stride, size = level
    pairs = []
    for device in range(count):
        digit = (device // stride) % size
        pairs.append((device, device + ((digit + step) % size - digit) * stride))
    return lax.ppermute(values, "dp", pairs)


def swapped(values):
    return lax.ppermute(values, "tensor", [(0, 1), (1, 0)])


def is_plain(count, rows):
    return levels_of(count) == [(4, 4), (2, 2), (1, 2)] and rows % 16 == 0


def after(values, *others):
    return lax.optimization_barrier((values, *others))[0]


class Gather:
    def __init__(self, shard, count, late=False, tail=False):
        self.count, self.levels, self.late, self.tail = count, levels_of(count), late, tail
        self.plain = is_plain(count, shard.shape[0])
        self.shard = shard
        if not self.plain:
            held = shard
            for level in self.levels:
                held = jnp.concatenate(
                    [held] + [shifted(held, count, level, step) for step in range(1, level[1])], axis=0
                )
            self.pieces = jnp.split(held, PIECES, axis=0)
            self.other = self.pieces[0]
        elif late:
            self.other = shifted(shard, count, self.levels[1], 1)
        else:
            self.received = self.along_first(shard)

    def along_first(self, rows):
        return [shifted(rows, self.count, self.levels[0], step) for step in range(1, 4)]

    def join_rows(self):
        if self.plain:
            self.shard = stack_rows([self.shard, self.other])

    def begin(self, other):
        if self.plain:
            self.shard = after(self.shard, other)
            self.received = self.along_first(self.shard)

    def stack(self, weight=0):
        if self.plain:
            _, second, third = self.levels
            if self.late:
                held, other = stack_rows([self.shard] + self.received, 2)
            else:
                held = stack_rows([self.shard] + self.received, weight=weight)
                other = self.other = shifted(held, self.count, second, 1)
            self.pieces = [held, other]
            if not self.tail:
                self.share()
        return self.pieces[0]

    def share(self, *others):
        if self.plain:
            self.pieces += [
                shifted(after(part, *others), self.count, self.levels[2], 1) for part in self.pieces
            ]


class Scatter:
    def __init__(self, kept, sent, count, rows):
        self.count, self.levels = count, levels_of(count)
        self.plain = is_plain(count, rows)
        if self.plain:
            self.own, self.other = kept, [shifted(part, count, self.levels[2], -1) for part in sent]
            return
        held = jnp.concatenate([jnp.concatenate(side, axis=1) for side in (kept, sent)], axis=0)
        for level in reversed(self.levels):
            size = level[1]
            pieces = held.reshape(size, held.shape[0] // size, held.shape[1])
            total = wide(pieces[0])
            for step in range(1, size):
                total = total + wide(shifted(pieces[step], count, level, -step))
            held = total if level == self.levels[0] else low(total)
        self.other, self.begun, self.parts = [held], held, [held]

    def second(self):
        if self.plain:
            self.own, sent = add_halves(self.own, self.other)
            self.other = [shifted(part, self.count, self.levels[1], -1) for part in sent]

    def third(self):
        if self.plain:
            pieces = add_split(self.own, self.other, 4)
            self.parts = [pieces[0]]
            for step in range(1, 4):
                self.parts.append(shifted(pieces[step], self.count, self.levels[0], -step))
            self.other, self.begun = self.parts[1:], pieces[0]

def placement(count, width):
    device = lax.axis_index("dp")
    place = jnp.arange(count)
    owner, weight = jnp.zeros_like(place), 1
    for stride, size in levels_of(count):
        step = (place // weight) % size
        owner = owner + ((device // stride) % size - step + size) % size * stride
        weight *= size
    rows = width // count
    natural = (owner[:, None] * rows + jnp.arange(rows)[None, :]).reshape(width)
    there = jnp.arange(width)
    return low(natural[None, :] == there[:, None]), low(natural[:, None] == there[None, :])


def spec(block, *place):
    return pl.BlockSpec(block, lambda step: place)


latest = []


def wait_for(*arrays):
    latest.extend(arrays)


def run(body, out_shapes, operands, specs=None, scratch=(), limit=LIMIT, last=False, weight=0):
    if last:
        limit = 60
        specs = [spec(array.shape, *[0] * array.ndim) for array in operands]
    grid = () if specs is None else (1,)
    specs = [None] * len(operands) if specs is None else specs
    specs = [
        pl.BlockSpec(memory_space=pltpu.VMEM) if given is None else given for given in specs
    ]
    count, waits = len(operands), len(latest)

    def ordered(*refs):
        body(*refs[:count], *refs[count + waits :])

    results = pl.pallas_call(
        ordered,
        out_shape=out_shapes,
        grid=grid,
        in_specs=specs + [pl.BlockSpec(memory_space=pl.ANY)] * waits,
        out_specs=[
            spec(shape.shape, *[0] * len(shape.shape)) if last else pl.BlockSpec(memory_space=pltpu.VMEM)
            for shape in out_shapes
        ],
        scratch_shapes=scratch,
        compiler_params=pltpu.CompilerParams(vmem_limit_bytes=limit * 1024 * 1024),
        cost_estimate=pl.CostEstimate(flops=weight, bytes_accessed=0, transcendentals=0),
    )(*operands, *latest)
    latest[:] = [min(results, key=lambda array: array.size)]
    return results


def half(*shape):
    return jax.ShapeDtypeStruct(shape, jnp.bfloat16)


def full(*shape):
    return jax.ShapeDtypeStruct(shape, jnp.float32)


def stack_rows(pieces, parts=1, weight=0):
    rows, width = pieces[0].shape
    rows //= parts

    def body(*refs):
        for number, ref in enumerate(refs[:-parts]):
            for part, out in enumerate(refs[-parts:]):
                out[number * rows : (number + 1) * rows, :] = ref[part * rows : (part + 1) * rows, :]

    stacked = run(body, [half(rows * len(pieces), width)] * parts, pieces, limit=SMALL, weight=weight)
    return stacked if parts > 1 else stacked[0]


def add_halves(left, right):
    rows = left[0].shape[0] // 2

    def body(*refs):
        pieces = len(left)
        for i in range(pieces):
            total = wide(refs[i][...]) + wide(refs[i + pieces][...])
            refs[i + 2 * pieces][...] = low(total[:rows])
            refs[i + 3 * pieces][...] = low(total[rows:])

    shapes = [half(rows, piece.shape[1]) for piece in left]
    results = run(body, shapes * 2, [*left, *right], limit=SMALL)
    return results[: len(left)], results[len(left) :]


def add_split(left, right, parts):
    rows = left[0].shape[0] // parts
    sizes = [piece.shape[1] for piece in left]

    def body(*refs):
        start = 0
        for i, size in enumerate(sizes):
            for number, out in enumerate(refs[2 * len(sizes) :]):
                part = slice(number * rows, (number + 1) * rows)
                total = wide(refs[i][part, :]) + wide(refs[i + len(sizes)][part, :])
                out[:, start : start + size] = low(total)
            start += size

    return run(body, [half(rows, sum(sizes))] * parts, [*left, *right], limit=SMALL)


def total_of(refs):
    total = wide(refs[0][...])
    for ref in refs[1:]:
        total = total + wide(ref[...])
    return total


def add_all(parts):
    def body(*refs):
        refs[-1][...] = total_of(refs[:-1])

    return run(body, [full(*parts[0].shape)], parts, limit=SMALL, weight=WEIGHT)[0]


def finish_feed_forward(total, weights, gains, hidden):
    rows, room = total.shape[0], total.shape[1] // 3

    def body(total_ref, weights_ref, gains_ref, sum_ref, down_ref, columns_ref):
        gain = gains_ref[:, :1]
        down_ref[...] = total_ref[:, 2 * room : 2 * room + hidden]
        sum_ref[0] = total_ref[:, :hidden] * gain
        sum_ref[1] = total_ref[:, room : room + hidden] * gain
        share = jnp.sum(wide(weights_ref[...]) * total_ref[:, : 2 * room], axis=1, keepdims=True) / gain
        lane = lax.broadcasted_iota(jnp.int32, (rows, 2), 1)
        columns_ref[...] = jnp.where(lane == 0, gains_ref[:, 1:], share)

    return run(
        body,
        [full(2, rows, hidden), full(rows, hidden), full(rows, 2)],
        [total, weights, gains],
        last=True,
    )


def finish_attention(parts, query_keys, values_out, columns):
    rows, inner = values_out.shape[0], values_out.shape[1] // 2

    def body(*refs):
        *parts, query_keys_ref, values_out_ref, columns_ref, sum_ref, out_ref, share_ref = refs
        total, gain = total_of(parts), columns_ref[:, :1]
        for number in range(3):
            sum_ref[number] = total[:, number * inner : (number + 1) * inner] * gain
        out_ref[...] = total[:, 3 * inner :]
        share = jnp.sum(wide(query_keys_ref[...]) * total[:, : 2 * inner], axis=1, keepdims=True)
        values = wide(values_out_ref[:, :inner]) * total[:, 2 * inner : 3 * inner]
        share = (share + jnp.sum(values, axis=1, keepdims=True)) / gain
        lane = lax.broadcasted_iota(jnp.int32, (rows, 2), 1)
        share_ref[...] = jnp.where(lane == 0, share, columns_ref[...])

    return run(
        body,
        [full(3, rows, inner), full(rows, inner), full(rows, 2)],
        [*parts, query_keys, values_out, columns],
        last=True,
    )


def normalize(values):
    average = jnp.mean(values, axis=-1, keepdims=True)
    centered = values - average
    variance = jnp.mean(centered * centered, axis=-1, keepdims=True)
    inverse = lax.rsqrt(variance + EPSILON)
    return centered * inverse, inverse


def norm_back(scaled, normed, inverse):
    first = jnp.mean(scaled, axis=-1, keepdims=True)
    second = jnp.mean(scaled * normed, axis=-1, keepdims=True)
    return inverse * (scaled - first - normed * second)


def partner(values):
    lane = lax.broadcasted_iota(jnp.int32, values.shape, 1)
    return jnp.where(
        lane % HD < HD // 2,
        pltpu.roll(values, LANES - HD // 2, 1),
        pltpu.roll(values, HD // 2, 1),
    )


def group(number):
    return slice(number * LANES, (number + 1) * LANES)


def rows_of(refs):
    return jnp.concatenate([ref[...] for ref in refs], axis=0)


def both_heads(values):
    lane = lax.broadcasted_iota(jnp.int32, values.shape, 1)
    nothing = jnp.zeros_like(values)
    return jnp.concatenate(
        [jnp.where(lane < HD, values, nothing), jnp.where(lane < HD, nothing, values)], axis=0
    )


def one_pair(values):
    rows = values.shape[0] // 2
    lane = lax.broadcasted_iota(jnp.int32, (rows, values.shape[1]), 1)
    return jnp.where(lane < HD, values[:rows], values[rows:])


def tiles_of(count, inner):
    for block in range(count // BLOCK):
        start = min(max(block * BLOCK - HALF, 0), count - WINDOW)
        for pair in range(inner // LANES):
            number = block * (inner // LANES) + pair
            yield number, pair, slice(block * BLOCK, (block + 1) * BLOCK), slice(start, start + WINDOW)


def prepare(tokens, cotangent, order):
    count, width = tokens.shape

    def body(tokens_ref, cotangent_ref, order_ref, inputs_ref, normed_ref, upstream_ref):
        inputs = product(tokens_ref[...], order_ref[...])
        inputs_ref[...] = low(inputs)
        normed_ref[...] = low(normalize(inputs)[0])
        upstream_ref[...] = low(product(cotangent_ref[...], order_ref[...]))

    return run(
        body, [half(count, width)] * 3, [tokens, cotangent, order]
    )


def attend_shares(normed, pieces, cosine, sine, column, row):
    count, width = normed.shape
    inner = pieces[0].shape[1] // 2
    tiles = list(tiles_of(count, inner))

    def body(normed_ref, a, b, c, d, cosine_ref, sine_ref, column_ref, row_ref, query_ref, keys_ref, shares_ref):
        projected = product(normed_ref[...], rows_of((a, b, c, d)))
        cosine, sine = cosine_ref[...], sine_ref[...]
        for number in range(inner // LANES):
            part = projected[:, group(number)]
            query_ref[:, group(number)] = low(part * cosine + partner(part) * sine)
            part = projected[:, group(number + inner // LANES)]
            keys_ref[:, group(number)] = low(part * cosine + partner(part) * sine)
        for number, pair, queries, window in tiles:
            if pair == 0:
                near = lax.broadcasted_iota(jnp.int32, (WINDOW, BLOCK), 0) + window.start
                near = near - lax.broadcasted_iota(jnp.int32, (WINDOW, BLOCK), 1) - queries.start
                allowed = (jnp.abs(near) <= HALF) & (column_ref[window, :] == row_ref[:, queries])
                allowed = jnp.concatenate([allowed.astype(jnp.float32)] * 2, axis=1) > 0.5
            query = both_heads(query_ref[queries, group(pair)])
            scores = product(keys_ref[window, group(pair)], query, NT) * SCALE
            scores = jnp.where(allowed, scores, MASKED)
            powers = jnp.exp(scores - jnp.max(scores, axis=0, keepdims=True))
            total = jnp.sum(powers, axis=0, keepdims=True)
            shares_ref[number] = low(powers * (1.0 / total))

    return run(
        body,
        [half(count, inner), half(count, inner), half(len(tiles), WINDOW, 2 * BLOCK)],
        [normed, *pieces, cosine, sine, column, row],
    )


def attend_values(normed, pieces, shares):
    count, width = normed.shape
    inner = pieces[0].shape[1] // 2
    tiles = list(tiles_of(count, inner))

    def body(normed_ref, a, b, c, d, shares_ref, values_ref, context_ref, out_ref):
        matrix = rows_of((a, b, c, d))
        values_ref[...] = low(product(normed_ref[...], matrix[:, :inner]))
        for number, pair, queries, window in tiles:
            both = product(shares_ref[number], values_ref[window, group(pair)], TN)
            context_ref[queries, group(pair)] = low(one_pair(both))
        out_ref[...] = low(product(context_ref[...], matrix[:, inner:], NT))

    return run(
        body,
        [half(count, inner), half(count, inner), half(count, width)],
        [normed, *pieces, shares],
    )


def feed_forward(inputs, upstream, own, other, gates_in, down):
    count, width = inputs.shape
    hidden = down[0].shape[1]

    def body(inputs_ref, upstream_ref, own_ref, other_ref, a, b, c, d, e, f, g, h,
             middle_ref, normed_ref, mixed_ref, gates_ref, forward_ref, back_ref):
        middle = wide(inputs_ref[...]) + (wide(own_ref[...]) + wide(other_ref[...]))
        middle_ref[...] = middle
        normed = low(normalize(middle)[0])
        normed_ref[...] = normed
        matrix, down = rows_of((a, b, c, d)), rows_of((e, f, g, h))
        gates = product(normed, matrix)
        active, factor = gates[:, :hidden], gates[:, hidden:]
        chance = 0.5 + 0.5 * lax.erf(active * 0.7071067811865476)
        bent = active * chance
        mixed = low(bent * factor)
        mixed_ref[...] = mixed
        forward_ref[...] = low(product(mixed, down, NT))
        grad_mixed = product(upstream_ref[...], down)
        slope = chance + active * (0.3989422804014327 * jnp.exp(-0.5 * active * active))
        gates_ref[:, :hidden] = low(grad_mixed * factor * slope)
        gates_ref[:, hidden:] = low(grad_mixed * bent)
        back_ref[...] = low(product(gates_ref[...], matrix, NT))

    return run(
        body,
        [full(count, width), half(count, width), half(count, hidden), half(count, 2 * hidden)]
        + [half(count, width)] * 2,
        [inputs, upstream, own, other, *gates_in, *down],
    )


def feed_forward_grads(normed, mixed, gates, upstream):
    count, width = upstream.shape
    hidden = mixed.shape[1]

    def body(normed_ref, mixed_ref, gates_ref, upstream_ref, *outs):
        for number in range(2):
            part = slice(number * width // 2, (number + 1) * width // 2)
            active_ref, factor_ref, down_ref = outs[3 * number : 3 * number + 3]
            both = product(normed_ref[:, part], gates_ref[...], TN)
            active_ref[...] = low(both[:, :hidden])
            factor_ref[...] = low(both[:, hidden:])
            down_ref[...] = low(product(upstream_ref[:, part], mixed_ref[...], TN))

    return run(body, [half(width // 2, hidden)] * 6, [normed, mixed, gates, upstream])


def add_output(middle, own, others, order):
    cut = others[0].shape[0]

    def body(middle_ref, own_ref, upper_ref, lower_ref, order_ref, out_ref):
        for part, ref in ((slice(0, cut), upper_ref), (slice(cut, None), lower_ref)):
            total = low(middle_ref[part, :] + (wide(own_ref[part, :]) + wide(ref[...])))
            out_ref[part, :] = low(product(total, order_ref[...]))

    return run(body, [half(*middle.shape)], [middle, own, *others, order], last=True)[0]


def attend_back_values(upstream, middle, own, other, pieces, context, shares):
    count, width = upstream.shape
    inner = context.shape[1]
    tiles = list(tiles_of(count, inner))

    def body(upstream_ref, middle_ref, own_ref, other_ref, a, b, c, d, context_ref, shares_ref,
             grad_middle_ref, branch_ref, grad_context_ref, grad_values_ref, total_ref):
        matrix = rows_of((a, b, c, d))
        normed, inverse = normalize(middle_ref[...])
        scaled = wide(own_ref[...]) + wide(other_ref[...])
        grad_middle = wide(upstream_ref[...]) + norm_back(scaled, normed, inverse)
        grad_middle_ref[...] = grad_middle
        branch_ref[...] = low(grad_middle)
        grad_context_ref[...] = low(product(branch_ref[...], matrix))
        total_ref[...] = jnp.zeros_like(total_ref)
        for number, pair, queries, window in tiles:
            upper = both_heads(grad_context_ref[queries, group(pair)])
            total_ref[window, group(pair)] += product(shares_ref[number], upper)
        grad_values_ref[...] = low(total_ref[...])

    return run(
        body,
        [full(count, width), half(count, width), half(count, inner), half(count, inner)],
        [upstream, middle, own, other, *pieces, context, shares],
        [None] * 4 + [spec((width // PIECES, inner), 0, 1)] * PIECES + [None] * 2,
        scratch=[pltpu.VMEM((count, inner), jnp.float32)],
    )


def attend_back_shares(query, keys, values, grad_context, shares, grad_values, cosine, sine, query_keys, values_out):
    count, inner = query.shape
    width = query_keys[0].shape[0] * PIECES
    tiles = list(tiles_of(count, inner))

    def body(query_ref, keys_ref, values_ref, grad_context_ref, shares_ref, grad_values_ref, cosine_ref, sine_ref,
             a, b, c, d, e, f, g, h, grad_ref, back_ref, total_ref):
        total_ref[...] = jnp.zeros_like(total_ref)
        cosine, sine = cosine_ref[...], sine_ref[...]
        for number, pair, queries, window in tiles:
            upper = both_heads(grad_context_ref[queries, group(pair)])
            grad_shares = product(values_ref[window, group(pair)], upper, NT)
            shares = wide(shares_ref[number])
            sums = jnp.sum(shares * grad_shares, axis=0, keepdims=True)
            grad_scores = low(shares * (grad_shares - sums))
            grad_query = one_pair(product(grad_scores, keys_ref[window, group(pair)], TN)) * SCALE
            grad_query = grad_query * cosine[queries] - partner(grad_query) * sine[queries]
            grad_ref[queries, group(pair)] = low(grad_query)
            lower = both_heads(query_ref[queries, group(pair)])
            total_ref[window, group(pair)] += product(grad_scores, lower)
        for pair in range(inner // LANES):
            grad_keys = total_ref[:, group(pair)] * SCALE
            grad_keys = grad_keys * cosine - partner(grad_keys) * sine
            grad_ref[:, group(pair + inner // LANES)] = low(grad_keys)
        back = product(grad_ref[...], rows_of((a, b, c, d)), NT)
        back_ref[...] = low(back + product(grad_values_ref[...], rows_of((e, f, g, h)), NT))

    return run(
        body,
        [half(count, 2 * inner), half(count, width)],
        [query, keys, values, grad_context, shares, grad_values, cosine, sine, *query_keys, *values_out],
        [None] * (8 + PIECES) + [spec((width // PIECES, inner), 0, 0)] * PIECES,
        scratch=[pltpu.VMEM((count, inner), jnp.float32)],
    )


def paired_grads(groups):
    pairs = [pair for group in groups for pair in group]
    count, width = pairs[0][0].shape
    sizes = [sum(right.shape[1] for _, right in group) for group in groups]

    def body(*refs):
        outs, number = refs[2 * len(pairs) :], 0
        for i, group in enumerate(groups):
            start = 0
            for _, right in group:
                size = right.shape[1]
                for side in range(2):
                    part = slice(side * width // 2, (side + 1) * width // 2)
                    both = product(refs[2 * number][:, part], refs[2 * number + 1][...], TN)
                    outs[2 * i + side][:, start : start + size] = low(both)
                start += size
                number += 1

    return run(
        body,
        [half(width // 2, size) for size in sizes for _ in range(2)],
        [array for pair in pairs for array in pair],
    )


def input_grads(grad_middle, inputs, own, other, order):
    count, width = inputs.shape

    def body(grad_middle_ref, inputs_ref, own_ref, other_ref, order_ref, out_ref):
        normed, inverse = normalize(wide(inputs_ref[...]))
        scaled = wide(own_ref[...]) + wide(other_ref[...])
        total = grad_middle_ref[...] + norm_back(scaled, normed, inverse)
        high = low(total)
        rest = low(total - wide(high))
        out_ref[...] = product(high, order_ref[...]) + product(rest, order_ref[...])

    return run(
        body,
        [full(count, width)],
        [grad_middle, inputs, own, other, order],
        last=True,
    )[0]


def rope_tables(positions):
    frequency = THETA ** (-jnp.arange(0, HD, 2).astype(jnp.float32) / HD)
    angle = positions.astype(jnp.float32)[:, None] * jnp.tile(frequency, LANES // (HD // 2))[None, :]
    sign = jnp.where(jnp.arange(LANES) % HD < HD // 2, -1.0, 1.0)
    return jnp.cos(angle), jnp.sin(angle) * sign[None, :]


def padded(values, width):
    return jnp.pad(values, ((0, 0), (0, width - values.shape[1])))


def per_device(
    devices, tokens, seg_ids, positions, gain_attn, w_qkv, w_attn_out, gain_mlp, w_in, w_mlp_out, cotangent
):
    width = tokens.shape[1]
    rows, _, inner = w_qkv.shape
    hidden = w_in.shape[2]
    room = -(-hidden // LANES) * LANES
    gain_one, gain_two = wide(gain_attn)[:, None], wide(gain_mlp)[:, None]
    scaled_qkv = [low(wide(w_qkv[:, i]) * gain_one) for i in range(3)]
    scaled_in = [padded(low(wide(w_in[:, i]) * gain_two), room) for i in range(2)]
    shard_one = jnp.concatenate(scaled_qkv[:2], axis=1)
    shard_two = jnp.concatenate([scaled_qkv[2], w_attn_out.T], axis=1)
    shard_three = jnp.concatenate(scaled_in, axis=1)
    shard_four = padded(w_mlp_out.T, room)
    latest.clear()
    query_keys = Gather(shard_one, devices)
    down = Gather(shard_four, devices, late=True)
    order, back = placement(devices, width)
    cosine, sine = rope_tables(positions)
    column, row = seg_ids[:, None], seg_ids[None, :]
    held = query_keys.stack()
    values_out = Gather(after(shard_two, held), devices)
    wait_for(query_keys.other)
    held = values_out.stack()
    gates_in = Gather(after(shard_three, held), devices, tail=True)
    wait_for(cosine, sine, column)
    inputs, normed_one, upstream = prepare(tokens, cotangent, order)
    down.join_rows()
    query, keys, shares = attend_shares(normed_one, query_keys.pieces, cosine, sine, column, row)
    wait_for(values_out.other)
    held = gates_in.stack(WEIGHT)
    down.begin(held)
    values, context, own = attend_values(normed_one, values_out.pieces, shares)
    other = swapped(own)
    wait_for(other)
    gates_in.share(down.stack())
    middle, normed_two, mixed, grad_gates, own_out, own_two = feed_forward(
        inputs, upstream, own, other, gates_in.pieces, down.pieces
    )
    other_two = swapped(own_two)
    grads_mlp = feed_forward_grads(normed_two, mixed, grad_gates, upstream)
    sums_mlp = Scatter(grads_mlp[:3], grads_mlp[3:], devices, rows)
    sums_mlp.second()
    early = own_out.shape[0] // EARLY
    upper_out = swapped(after(own_out[:early], other_two))
    grad_middle, branch, grad_context, grad_values = attend_back_values(
        upstream, middle, own_two, other_two, values_out.pieces, context, shares
    )
    grad_query_keys, own_one = attend_back_shares(
        query, keys, values, grad_context, shares, grad_values, cosine, sine, query_keys.pieces, values_out.pieces
    )
    other_one = swapped(own_one)
    wait_for(upper_out, *sums_mlp.other)
    kept, sent = paired_grads(
        [[(normed_one, grad_query_keys), (normed_one, grad_values), (branch, context)]]
    )
    sums = Scatter([kept], [sent], devices, rows)
    sums_mlp.third()
    sums.second()
    wait_for(other_one)
    sum_mlp = add_all(sums_mlp.parts)
    sums.third()
    lower_out = swapped(after(own_out[early:], sums.begun))
    sum_in, sum_down, columns = finish_feed_forward(
        sum_mlp, shard_three, jnp.concatenate([gain_two, gain_one], axis=1), hidden
    )
    grad_input = input_grads(grad_middle, inputs, own_one, other_one, back)
    sum_qkv, sum_out, share = finish_attention(sums.parts, shard_one, shard_two, columns)
    output = add_output(middle, own_out, (upper_out, lower_out), back)
    gains = after(share, output) + swapped(share)
    sum_qkv, sum_in = (jnp.transpose(array, (1, 0, 2)) for array in (sum_qkv, sum_in))
    return (output, grad_input, gains[:, 0], sum_qkv, sum_out.T, gains[:, 1], sum_in, sum_down.T)


def solution(mesh):
    return jax.shard_map(
        functools.partial(per_device, mesh.shape["dp"]),
        mesh=mesh,
        in_specs=(
            P("dp", None),
            P("dp"),
            P("dp"),
            P("dp"),
            P("dp", None, "tensor"),
            P("tensor", "dp"),
            P("dp"),
            P("dp", None, "tensor"),
            P("tensor", "dp"),
            P("dp", None),
        ),
        out_specs=(
            P("dp", None),
            P("dp", None),
            P("dp"),
            P("dp", None, "tensor"),
            P("tensor", "dp"),
            P("dp"),
            P("dp", None, "tensor"),
            P("tensor", "dp"),
        ),
        check_vma=False,
    )
```

```python
import functools

import jax
import jax.numpy as jnp
from jax import lax
from jax.experimental import pallas as pl
from jax.experimental.pallas import tpu as pltpu
from jax.sharding import PartitionSpec as P

HD = 64
HALF = 64
LIMIT = 16
SMALL = 4
LANES = 128
BLOCK = 128
WINDOW = 256
EARLY = 2
WEIGHT = 10**10
PIECES = 4

EPSILON = 1e-05
THETA = 10000.0
MASKED = -1e30
SCALE = HD ** (-0.5)

NN = (((1,), (0,)), ((), ()))
NT = (((1,), (1,)), ((), ()))
TN = (((0,), (0,)), ((), ()))


def product(left, right, dims=NN):
    return lax.dot_general(left, right, dims, preferred_element_type=jnp.float32)


def low(values):
    return values.astype(jnp.bfloat16)


def wide(values):
    return values.astype(jnp.float32)


def levels_of(count):
    levels, stride = [], count
    while stride > 1:
        size = 4 if stride % 8 == 0 else 2 if stride % 2 == 0 else stride
        stride //= size
        levels.append((stride, size))
    return levels


def shifted(values, count, level, step):
    stride, size = level
    pairs = []
    for device in range(count):
        digit = (device // stride) % size
        pairs.append((device, device + ((digit + step) % size - digit) * stride))
    return lax.ppermute(values, "dp", pairs)


def swapped(values):
    return lax.ppermute(values, "tensor", [(0, 1), (1, 0)])


def is_plain(count, rows):
    return levels_of(count) == [(4, 4), (2, 2), (1, 2)] and rows % 16 == 0


def after(values, *others):
    return lax.optimization_barrier((values, *others))[0]


class Gather:
    def __init__(self, shard, count, late=False, tail=False):
        self.count, self.levels, self.late, self.tail = count, levels_of(count), late, tail
        self.plain = is_plain(count, shard.shape[0])
        self.shard = shard
        if not self.plain:
            held = shard
            for level in self.levels:
                held = jnp.concatenate(
                    [held] + [shifted(held, count, level, step) for step in range(1, level[1])], axis=0
                )
            self.pieces = jnp.split(held, PIECES, axis=0)
            self.other = self.pieces[0]
        elif late:
            self.other = shifted(shard, count, self.levels[1], 1)
        else:
            self.received = self.along_first(shard)

    def along_first(self, rows):
        return [shifted(rows, self.count, self.levels[0], step) for step in range(1, 4)]

    def join_rows(self):
        if self.plain:
            self.shard = stack_rows([self.shard, self.other])

    def begin(self, other):
        if self.plain:
            self.shard = after(self.shard, other)
            self.received = self.along_first(self.shard)

    def stack(self, weight=0):
        if self.plain:
            _, second, third = self.levels
            if self.late:
                held, other = stack_rows([self.shard] + self.received, 2, weight)
            else:
                held = stack_rows([self.shard] + self.received, weight=weight)
                other = self.other = shifted(held, self.count, second, 1)
            self.pieces = [held, other]
            if not self.tail:
                self.share()
        return self.pieces[0]

    def share(self, *others):
        if self.plain:
            self.pieces += [
                shifted(after(part, *(array for array in others if array is not part)), self.count, self.levels[2], 1)
                for part in self.pieces
            ]


class Scatter:
    def __init__(self, kept, sent, count, rows):
        self.count, self.levels = count, levels_of(count)
        self.plain = is_plain(count, rows)
        if self.plain:
            self.own, self.other = kept, [shifted(part, count, self.levels[2], -1) for part in sent]
            return
        held = jnp.concatenate([jnp.concatenate(side, axis=1) for side in (kept, sent)], axis=0)
        for level in reversed(self.levels):
            size = level[1]
            pieces = held.reshape(size, held.shape[0] // size, held.shape[1])
            total = wide(pieces[0])
            for step in range(1, size):
                total = total + wide(shifted(pieces[step], count, level, -step))
            held = total if level == self.levels[0] else low(total)
        self.other, self.begun, self.parts = [held], held, [held]

    def second(self):
        if self.plain:
            self.own, sent = add_halves(self.own, self.other)
            self.other = [shifted(part, self.count, self.levels[1], -1) for part in sent]

    def third(self):
        if self.plain:
            pieces = add_split(self.own, self.other, 4)
            self.parts = [pieces[0]]
            for step in range(1, 4):
                self.parts.append(shifted(pieces[step], self.count, self.levels[0], -step))
            self.other, self.begun = self.parts[1:], pieces[0]

def placement(count, width):
    device = lax.axis_index("dp")
    place = jnp.arange(count)
    owner, weight = jnp.zeros_like(place), 1
    for stride, size in levels_of(count):
        step = (place // weight) % size
        owner = owner + ((device // stride) % size - step + size) % size * stride
        weight *= size
    rows = width // count
    natural = (owner[:, None] * rows + jnp.arange(rows)[None, :]).reshape(width)
    there = jnp.arange(width)
    return low(natural[None, :] == there[:, None]), low(natural[:, None] == there[None, :])


def spec(block, *place):
    return pl.BlockSpec(block, lambda step: place)


latest = []


def wait_for(*arrays):
    latest.extend(arrays)


def run(body, out_shapes, operands, specs=None, scratch=(), limit=LIMIT, last=False, weight=0):
    if last:
        limit = 60
        specs = [spec(array.shape, *[0] * array.ndim) for array in operands]
    grid = () if specs is None else (1,)
    specs = [None] * len(operands) if specs is None else specs
    specs = [
        pl.BlockSpec(memory_space=pltpu.VMEM) if given is None else given for given in specs
    ]
    count, waits = len(operands), len(latest)

    def ordered(*refs):
        body(*refs[:count], *refs[count + waits :])

    results = pl.pallas_call(
        ordered,
        out_shape=out_shapes,
        grid=grid,
        in_specs=specs + [pl.BlockSpec(memory_space=pl.ANY)] * waits,
        out_specs=[
            spec(shape.shape, *[0] * len(shape.shape)) if last else pl.BlockSpec(memory_space=pltpu.VMEM)
            for shape in out_shapes
        ],
        scratch_shapes=scratch,
        compiler_params=pltpu.CompilerParams(vmem_limit_bytes=limit * 1024 * 1024),
        cost_estimate=pl.CostEstimate(flops=weight, bytes_accessed=0, transcendentals=0),
    )(*operands, *latest)
    latest[:] = [min(results, key=lambda array: array.size)]
    return results


def half(*shape):
    return jax.ShapeDtypeStruct(shape, jnp.bfloat16)


def full(*shape):
    return jax.ShapeDtypeStruct(shape, jnp.float32)


def stack_rows(pieces, parts=1, weight=0):
    rows, width = pieces[0].shape
    rows //= parts

    def body(*refs):
        for number, ref in enumerate(refs[:-parts]):
            for part, out in enumerate(refs[-parts:]):
                out[number * rows : (number + 1) * rows, :] = ref[part * rows : (part + 1) * rows, :]

    stacked = run(body, [half(rows * len(pieces), width)] * parts, pieces, limit=SMALL, weight=weight)
    return stacked if parts > 1 else stacked[0]


def add_halves(left, right):
    rows = left[0].shape[0] // 2

    def body(*refs):
        pieces = len(left)
        for i in range(pieces):
            total = wide(refs[i][...]) + wide(refs[i + pieces][...])
            refs[i + 2 * pieces][...] = low(total[:rows])
            refs[i + 3 * pieces][...] = low(total[rows:])

    shapes = [half(rows, piece.shape[1]) for piece in left]
    results = run(body, shapes * 2, [*left, *right], limit=SMALL)
    return results[: len(left)], results[len(left) :]


def add_split(left, right, parts):
    rows = left[0].shape[0] // parts
    sizes = [piece.shape[1] for piece in left]

    def body(*refs):
        start = 0
        for i, size in enumerate(sizes):
            for number, out in enumerate(refs[2 * len(sizes) :]):
                part = slice(number * rows, (number + 1) * rows)
                total = wide(refs[i][part, :]) + wide(refs[i + len(sizes)][part, :])
                out[:, start : start + size] = low(total)
            start += size

    return run(body, [half(rows, sum(sizes))] * parts, [*left, *right], limit=SMALL)


def total_of(refs):
    total = wide(refs[0][...])
    for ref in refs[1:]:
        total = total + wide(ref[...])
    return total


def add_all(parts):
    def body(*refs):
        refs[-1][...] = total_of(refs[:-1])

    return run(body, [full(*parts[0].shape)], parts, limit=SMALL, weight=WEIGHT)[0]


def finish_feed_forward(total, weights, gains, hidden):
    rows, room = total.shape[0], total.shape[1] // 3

    def body(total_ref, weights_ref, gains_ref, sum_ref, down_ref, columns_ref):
        gain = gains_ref[:, :1]
        down_ref[...] = total_ref[:, 2 * room : 2 * room + hidden]
        sum_ref[:, 0, :] = total_ref[:, :hidden] * gain
        sum_ref[:, 1, :] = total_ref[:, room : room + hidden] * gain
        share = jnp.sum(wide(weights_ref[...]) * total_ref[:, : 2 * room], axis=1, keepdims=True) / gain
        lane = lax.broadcasted_iota(jnp.int32, (rows, 2), 1)
        columns_ref[...] = jnp.where(lane == 0, gains_ref[:, 1:], share)

    return run(
        body,
        [full(rows, 2, hidden), full(rows, hidden), full(rows, 2)],
        [total, weights, gains],
        last=True,
    )


def finish_attention(parts, query_keys, values_out, columns):
    rows, inner = values_out.shape[0], values_out.shape[1] // 2

    def body(*refs):
        *parts, query_keys_ref, values_out_ref, columns_ref, sum_ref, out_ref, share_ref = refs
        total, gain = total_of(parts), columns_ref[:, :1]
        for number in range(3):
            sum_ref[number] = total[:, number * inner : (number + 1) * inner] * gain
        out_ref[...] = total[:, 3 * inner :]
        share = jnp.sum(wide(query_keys_ref[...]) * total[:, : 2 * inner], axis=1, keepdims=True)
        values = wide(values_out_ref[:, :inner]) * total[:, 2 * inner : 3 * inner]
        share = (share + jnp.sum(values, axis=1, keepdims=True)) / gain
        place = lax.broadcasted_iota(jnp.int32, (rows, rows), 0) == lax.broadcasted_iota(jnp.int32, (rows, rows), 1)
        for number, column in enumerate((share, columns_ref[:, 1:])):
            spread = jnp.where(place, column, jnp.zeros((rows, rows), jnp.float32))
            share_ref[number : number + 1, :] = jnp.sum(spread, axis=0, keepdims=True)

    return run(
        body,
        [full(3, rows, inner), full(rows, inner), full(2, rows)],
        [*parts, query_keys, values_out, columns],
        last=True,
    )


def normalize(values):
    average = jnp.mean(values, axis=-1, keepdims=True)
    centered = values - average
    variance = jnp.mean(centered * centered, axis=-1, keepdims=True)
    inverse = lax.rsqrt(variance + EPSILON)
    return centered * inverse, inverse


def norm_back(scaled, normed, inverse):
    first = jnp.mean(scaled, axis=-1, keepdims=True)
    second = jnp.mean(scaled * normed, axis=-1, keepdims=True)
    return inverse * (scaled - first - normed * second)


def partner(values):
    lane = lax.broadcasted_iota(jnp.int32, values.shape, 1)
    return jnp.where(
        lane % HD < HD // 2,
        pltpu.roll(values, LANES - HD // 2, 1),
        pltpu.roll(values, HD // 2, 1),
    )


def group(number):
    return slice(number * LANES, (number + 1) * LANES)


def rows_of(refs):
    return jnp.concatenate([ref[...] for ref in refs], axis=0)


def both_heads(values):
    lane = lax.broadcasted_iota(jnp.int32, values.shape, 1)
    nothing = jnp.zeros_like(values)
    return jnp.concatenate(
        [jnp.where(lane < HD, values, nothing), jnp.where(lane < HD, nothing, values)], axis=0
    )


def one_pair(values):
    rows = values.shape[0] // 2
    lane = lax.broadcasted_iota(jnp.int32, (rows, values.shape[1]), 1)
    return jnp.where(lane < HD, values[:rows], values[rows:])


def tiles_of(count, inner):
    for block in range(count // BLOCK):
        start = min(max(block * BLOCK - HALF, 0), count - WINDOW)
        for pair in range(inner // LANES):
            number = block * (inner // LANES) + pair
            yield number, pair, slice(block * BLOCK, (block + 1) * BLOCK), slice(start, start + WINDOW)


def prepare(tokens, order):
    def body(tokens_ref, order_ref, inputs_ref, normed_ref):
        inputs = product(tokens_ref[...], order_ref[...])
        inputs_ref[...] = low(inputs)
        normed_ref[...] = low(normalize(inputs)[0])

    return run(body, [half(*tokens.shape)] * 2, [tokens, order])


def reorder(values, order):
    def body(values_ref, order_ref, out_ref):
        out_ref[...] = low(product(values_ref[...], order_ref[...]))

    return run(body, [half(*values.shape)], [values, order])[0]


def attend_shares(normed, pieces, cosine, sine, column, row):
    count, width = normed.shape
    inner = pieces[0].shape[1] // 2
    tiles = list(tiles_of(count, inner))

    def body(normed_ref, a, b, c, d, cosine_ref, sine_ref, column_ref, row_ref, query_ref, keys_ref, shares_ref):
        projected = product(normed_ref[...], rows_of((a, b, c, d)))
        cosine, sine = cosine_ref[...], sine_ref[...]
        for number in range(inner // LANES):
            part = projected[:, group(number)]
            query_ref[:, group(number)] = low(part * cosine + partner(part) * sine)
            part = projected[:, group(number + inner // LANES)]
            keys_ref[:, group(number)] = low(part * cosine + partner(part) * sine)
        for number, pair, queries, window in tiles:
            if pair == 0:
                near = lax.broadcasted_iota(jnp.int32, (WINDOW, BLOCK), 0) + window.start
                near = near - lax.broadcasted_iota(jnp.int32, (WINDOW, BLOCK), 1) - queries.start
                allowed = (jnp.abs(near) <= HALF) & (column_ref[window, :] == row_ref[:, queries])
                allowed = jnp.concatenate([allowed.astype(jnp.float32)] * 2, axis=1) > 0.5
            query = both_heads(query_ref[queries, group(pair)])
            scores = product(keys_ref[window, group(pair)], query, NT) * SCALE
            scores = jnp.where(allowed, scores, MASKED)
            powers = jnp.exp(scores - jnp.max(scores, axis=0, keepdims=True))
            total = jnp.sum(powers, axis=0, keepdims=True)
            shares_ref[number] = low(powers * (1.0 / total))

    return run(
        body,
        [half(count, inner), half(count, inner), half(len(tiles), WINDOW, 2 * BLOCK)],
        [normed, *pieces, cosine, sine, column, row],
    )


def attend_values(normed, pieces, shares):
    count, width = normed.shape
    inner = pieces[0].shape[1] // 2
    tiles = list(tiles_of(count, inner))

    def body(normed_ref, a, b, c, d, shares_ref, values_ref, context_ref, out_ref):
        matrix = rows_of((a, b, c, d))
        values_ref[...] = low(product(normed_ref[...], matrix[:, :inner]))
        for number, pair, queries, window in tiles:
            both = product(shares_ref[number], values_ref[window, group(pair)], TN)
            context_ref[queries, group(pair)] = low(one_pair(both))
        out_ref[...] = low(product(context_ref[...], matrix[:, inner:], NT))

    return run(
        body,
        [half(count, inner), half(count, inner), half(count, width)],
        [normed, *pieces, shares],
    )


def settle(inputs, own, other):
    def body(inputs_ref, own_ref, other_ref, middle_ref, normed_ref):
        middle = wide(inputs_ref[...]) + (wide(own_ref[...]) + wide(other_ref[...]))
        middle_ref[...] = middle
        normed_ref[...] = low(normalize(middle)[0])

    return run(body, [full(*inputs.shape), half(*inputs.shape)], [inputs, own, other], weight=WEIGHT)


def feed_forward(normed, upstream, gates_in, down):
    count, width = normed.shape
    hidden = down[0].shape[1]

    def body(normed_ref, upstream_ref, a, b, c, d, e, f, g, h,
             mixed_ref, gates_ref, forward_ref, back_ref):
        matrix, down = rows_of((a, b, c, d)), rows_of((e, f, g, h))
        gates = product(normed_ref[...], matrix)
        active, factor = gates[:, :hidden], gates[:, hidden:]
        chance = 0.5 + 0.5 * lax.erf(active * 0.7071067811865476)
        bent = active * chance
        mixed = low(bent * factor)
        mixed_ref[...] = mixed
        forward_ref[...] = low(product(mixed, down, NT))
        grad_mixed = product(upstream_ref[...], down)
        slope = chance + active * (0.3989422804014327 * jnp.exp(-0.5 * active * active))
        gates_ref[:, :hidden] = low(grad_mixed * factor * slope)
        gates_ref[:, hidden:] = low(grad_mixed * bent)
        back_ref[...] = low(product(gates_ref[...], matrix, NT))

    return run(
        body,
        [half(count, hidden), half(count, 2 * hidden), half(count, width), half(count, width)],
        [normed, upstream, *gates_in, *down],
    )


def feed_forward_grads(normed, mixed, gates, upstream):
    count, width = upstream.shape
    hidden = mixed.shape[1]

    def body(normed_ref, mixed_ref, gates_ref, upstream_ref, *outs):
        for number in range(2):
            part = slice(number * width // 2, (number + 1) * width // 2)
            active_ref, factor_ref, down_ref = outs[3 * number : 3 * number + 3]
            both = product(normed_ref[:, part], gates_ref[...], TN)
            active_ref[...] = low(both[:, :hidden])
            factor_ref[...] = low(both[:, hidden:])
            down_ref[...] = low(product(upstream_ref[:, part], mixed_ref[...], TN))

    return run(body, [half(width // 2, hidden)] * 6, [normed, mixed, gates, upstream])


def add_output(middle, own, others, order):
    cut = others[0].shape[0]

    def body(middle_ref, own_ref, upper_ref, lower_ref, order_ref, out_ref):
        for part, ref in ((slice(0, cut), upper_ref), (slice(cut, None), lower_ref)):
            total = low(middle_ref[part, :] + (wide(own_ref[part, :]) + wide(ref[...])))
            out_ref[part, :] = low(product(total, order_ref[...]))

    return run(body, [half(*middle.shape)], [middle, own, *others, order])[0]


def attend_back_values(upstream, middle, own, other, pieces, context, shares):
    count, width = upstream.shape
    inner = context.shape[1]
    tiles = list(tiles_of(count, inner))

    def body(upstream_ref, middle_ref, own_ref, other_ref, a, b, c, d, context_ref, shares_ref,
             grad_middle_ref, branch_ref, grad_context_ref, grad_values_ref, total_ref):
        matrix = rows_of((a, b, c, d))
        normed, inverse = normalize(middle_ref[...])
        scaled = wide(own_ref[...]) + wide(other_ref[...])
        grad_middle = wide(upstream_ref[...]) + norm_back(scaled, normed, inverse)
        grad_middle_ref[...] = grad_middle
        branch_ref[...] = low(grad_middle)
        grad_context_ref[...] = low(product(branch_ref[...], matrix))
        total_ref[...] = jnp.zeros_like(total_ref)
        for number, pair, queries, window in tiles:
            upper = both_heads(grad_context_ref[queries, group(pair)])
            total_ref[window, group(pair)] += product(shares_ref[number], upper)
        grad_values_ref[...] = low(total_ref[...])

    return run(
        body,
        [full(count, width), half(count, width), half(count, inner), half(count, inner)],
        [upstream, middle, own, other, *pieces, context, shares],
        [None] * 4 + [spec((width // PIECES, inner), 0, 1)] * PIECES + [None] * 2,
        scratch=[pltpu.VMEM((count, inner), jnp.float32)],
    )


def attend_back_shares(query, keys, values, grad_context, shares, grad_values, cosine, sine, query_keys, values_out):
    count, inner = query.shape
    width = query_keys[0].shape[0] * PIECES
    tiles = list(tiles_of(count, inner))

    def body(query_ref, keys_ref, values_ref, grad_context_ref, shares_ref, grad_values_ref, cosine_ref, sine_ref,
             a, b, c, d, e, f, g, h, grad_ref, back_ref, total_ref):
        total_ref[...] = jnp.zeros_like(total_ref)
        cosine, sine = cosine_ref[...], sine_ref[...]
        for number, pair, queries, window in tiles:
            upper = both_heads(grad_context_ref[queries, group(pair)])
            grad_shares = product(values_ref[window, group(pair)], upper, NT)
            shares = wide(shares_ref[number])
            sums = jnp.sum(shares * grad_shares, axis=0, keepdims=True)
            grad_scores = low(shares * (grad_shares - sums))
            grad_query = one_pair(product(grad_scores, keys_ref[window, group(pair)], TN)) * SCALE
            grad_query = grad_query * cosine[queries] - partner(grad_query) * sine[queries]
            grad_ref[queries, group(pair)] = low(grad_query)
            lower = both_heads(query_ref[queries, group(pair)])
            total_ref[window, group(pair)] += product(grad_scores, lower)
        for pair in range(inner // LANES):
            grad_keys = total_ref[:, group(pair)] * SCALE
            grad_keys = grad_keys * cosine - partner(grad_keys) * sine
            grad_ref[:, group(pair + inner // LANES)] = low(grad_keys)
        back = product(grad_ref[...], rows_of((a, b, c, d)), NT)
        back_ref[...] = low(back + product(grad_values_ref[...], rows_of((e, f, g, h)), NT))

    return run(
        body,
        [half(count, 2 * inner), half(count, width)],
        [query, keys, values, grad_context, shares, grad_values, cosine, sine, *query_keys, *values_out],
        [None] * (8 + PIECES) + [spec((width // PIECES, inner), 0, 0)] * PIECES,
        scratch=[pltpu.VMEM((count, inner), jnp.float32)],
    )


def paired_grads(groups):
    pairs = [pair for group in groups for pair in group]
    count, width = pairs[0][0].shape
    sizes = [sum(right.shape[1] for _, right in group) for group in groups]

    def body(*refs):
        outs, number = refs[2 * len(pairs) :], 0
        for i, group in enumerate(groups):
            start = 0
            for _, right in group:
                size = right.shape[1]
                for side in range(2):
                    part = slice(side * width // 2, (side + 1) * width // 2)
                    both = product(refs[2 * number][:, part], refs[2 * number + 1][...], TN)
                    outs[2 * i + side][:, start : start + size] = low(both)
                start += size
                number += 1

    return run(
        body,
        [half(width // 2, size) for size in sizes for _ in range(2)],
        [array for pair in pairs for array in pair],
    )


def input_grads(grad_middle, inputs, own, other, order):
    count, width = inputs.shape

    def body(grad_middle_ref, inputs_ref, own_ref, other_ref, order_ref, out_ref):
        normed, inverse = normalize(wide(inputs_ref[...]))
        scaled = wide(own_ref[...]) + wide(other_ref[...])
        total = grad_middle_ref[...] + norm_back(scaled, normed, inverse)
        high = low(total)
        rest = low(total - wide(high))
        out_ref[...] = product(high, order_ref[...]) + product(rest, order_ref[...])

    return run(
        body,
        [full(count, width)],
        [grad_middle, inputs, own, other, order],
        last=True,
    )[0]


def rope_tables(positions):
    frequency = THETA ** (-jnp.arange(0, HD, 2).astype(jnp.float32) / HD)
    angle = positions.astype(jnp.float32)[:, None] * jnp.tile(frequency, LANES // (HD // 2))[None, :]
    sign = jnp.where(jnp.arange(LANES) % HD < HD // 2, -1.0, 1.0)
    return jnp.cos(angle), jnp.sin(angle) * sign[None, :]


def padded(values, width):
    return jnp.pad(values, ((0, 0), (0, width - values.shape[1])))


def per_device(
    devices, tokens, seg_ids, positions, gain_attn, w_qkv, w_attn_out, gain_mlp, w_in, w_mlp_out, cotangent
):
    width = tokens.shape[1]
    rows, _, inner = w_qkv.shape
    hidden = w_in.shape[2]
    room = -(-hidden // LANES) * LANES
    gain_one, gain_two = wide(gain_attn)[:, None], wide(gain_mlp)[:, None]
    scaled_qkv = [low(wide(w_qkv[:, i]) * gain_one) for i in range(3)]
    scaled_in = [padded(low(wide(w_in[:, i]) * gain_two), room) for i in range(2)]
    shard_one = jnp.concatenate(scaled_qkv[:2], axis=1)
    shard_two = jnp.concatenate([scaled_qkv[2], w_attn_out.T], axis=1)
    shard_three = jnp.concatenate(scaled_in, axis=1)
    shard_four = padded(w_mlp_out.T, room)
    latest.clear()
    query_keys = Gather(shard_one, devices)
    down = Gather(shard_four, devices, late=True)
    order, back = placement(devices, width)
    cosine, sine = rope_tables(positions)
    column, row = seg_ids[:, None], seg_ids[None, :]
    held = query_keys.stack()
    values_out = Gather(after(shard_two, held), devices)
    inputs, normed_one = prepare(tokens, order)
    wait_for(query_keys.other)
    held = values_out.stack()
    gates_in = Gather(after(shard_three, held), devices, tail=True)
    wait_for(cosine, sine, column)
    down.join_rows()
    query, keys, shares = attend_shares(normed_one, query_keys.pieces, cosine, sine, column, row)
    wait_for(values_out.other)
    held = gates_in.stack(WEIGHT)
    down.begin(held)
    values, context, own = attend_values(normed_one, values_out.pieces, shares)
    other = swapped(own)
    upstream = reorder(cotangent, order)
    down.stack()
    gates_in.share(gates_in.other)
    middle, normed_two = settle(inputs, own, other)
    mixed, grad_gates, own_out, own_two = feed_forward(
        normed_two, upstream, gates_in.pieces, down.pieces
    )
    other_two = swapped(own_two)
    grads_mlp = feed_forward_grads(normed_two, mixed, grad_gates, upstream)
    sums_mlp = Scatter(grads_mlp[:3], grads_mlp[3:], devices, rows)
    sums_mlp.second()
    early = own_out.shape[0] // EARLY
    upper_out = swapped(own_out[:early])
    grad_middle, branch, grad_context, grad_values = attend_back_values(
        upstream, middle, own_two, other_two, values_out.pieces, context, shares
    )
    grad_query_keys, own_one = attend_back_shares(
        query, keys, values, grad_context, shares, grad_values, cosine, sine, query_keys.pieces, values_out.pieces
    )
    other_one = swapped(own_one)
    wait_for(upper_out, *sums_mlp.other)
    kept, sent = paired_grads(
        [[(normed_one, grad_query_keys), (normed_one, grad_values), (branch, context)]]
    )
    sums = Scatter([kept], [sent], devices, rows)
    sums_mlp.third()
    sums.second()
    wait_for(other_one)
    sum_mlp = add_all(sums_mlp.parts)
    sums.third()
    lower_out = swapped(after(own_out[early:], sums.begun))
    sum_in, sum_down, columns = finish_feed_forward(
        sum_mlp, shard_three, jnp.concatenate([gain_two, gain_one], axis=1), hidden
    )
    grad_input = input_grads(grad_middle, inputs, own_one, other_one, back)
    output = add_output(middle, own_out, (upper_out, lower_out), back)
    sum_qkv, sum_out, share = finish_attention(sums.parts, shard_one, shard_two, columns)
    gains = after(share, output) + swapped(share)
    sum_qkv = jnp.transpose(sum_qkv, (1, 0, 2))
    return (output, grad_input, gains[0], sum_qkv, sum_out.T, gains[1], sum_in, sum_down.T)


def solution(mesh):
    return jax.shard_map(
        functools.partial(per_device, mesh.shape["dp"]),
        mesh=mesh,
        in_specs=(
            P("dp", None),
            P("dp"),
            P("dp"),
            P("dp"),
            P("dp", None, "tensor"),
            P("tensor", "dp"),
            P("dp"),
            P("dp", None, "tensor"),
            P("tensor", "dp"),
            P("dp", None),
        ),
        out_specs=(
            P("dp", None),
            P("dp", None),
            P("dp"),
            P("dp", None, "tensor"),
            P("tensor", "dp"),
            P("dp"),
            P("dp", None, "tensor"),
            P("tensor", "dp"),
        ),
        check_vma=False,
    )
```

```python
import functools

import jax
import jax.numpy as jnp
from jax import lax
from jax.experimental import pallas as pl
from jax.experimental.pallas import tpu as pltpu
from jax.sharding import PartitionSpec as P

HD = 64
HALF = 64
LIMIT = 16
SMALL = 4
LANES = 128
BLOCK = 128
WINDOW = 256
EARLY = 2
WEIGHT = 10**10
PIECES = 4

EPSILON = 1e-05
THETA = 10000.0
MASKED = -1e30
SCALE = HD ** (-0.5)

NN = (((1,), (0,)), ((), ()))
NT = (((1,), (1,)), ((), ()))
TN = (((0,), (0,)), ((), ()))


def product(left, right, dims=NN):
    return lax.dot_general(left, right, dims, preferred_element_type=jnp.float32)


def low(values):
    return values.astype(jnp.bfloat16)


def wide(values):
    return values.astype(jnp.float32)


def levels_of(count):
    levels, stride = [], count
    while stride > 1:
        size = 4 if stride % 8 == 0 else 2 if stride % 2 == 0 else stride
        stride //= size
        levels.append((stride, size))
    return levels


def shifted(values, count, level, step):
    stride, size = level
    pairs = []
    for device in range(count):
        digit = (device // stride) % size
        pairs.append((device, device + ((digit + step) % size - digit) * stride))
    return lax.ppermute(values, "dp", pairs)


def swapped(values):
    return lax.ppermute(values, "tensor", [(0, 1), (1, 0)])


def is_plain(count, rows):
    return levels_of(count) == [(4, 4), (2, 2), (1, 2)] and rows % 16 == 0


def after(values, *others):
    return lax.optimization_barrier((values, *others))[0]


class Gather:
    def __init__(self, shard, count, late=False, tail=False):
        self.count, self.levels, self.late, self.tail = count, levels_of(count), late, tail
        self.plain = is_plain(count, shard.shape[0])
        self.shard = shard
        if not self.plain:
            held = shard
            for level in self.levels:
                held = jnp.concatenate(
                    [held] + [shifted(held, count, level, step) for step in range(1, level[1])], axis=0
                )
            self.pieces = jnp.split(held, PIECES, axis=0)
            self.other = self.pieces[0]
        elif late:
            self.other = shifted(shard, count, self.levels[1], 1)
        else:
            self.received = self.along_first(shard)

    def along_first(self, rows):
        return [shifted(rows, self.count, self.levels[0], step) for step in range(1, 4)]

    def join_rows(self):
        if self.plain:
            self.shard = stack_rows([self.shard, self.other])

    def begin(self, other):
        if self.plain:
            self.shard = after(self.shard, other)
            self.received = self.along_first(self.shard)

    def stack(self, weight=0):
        if self.plain:
            _, second, third = self.levels
            if self.late:
                held, other = stack_rows([self.shard] + self.received, 2, weight)
            else:
                held = stack_rows([self.shard] + self.received, weight=weight)
                other = self.other = shifted(held, self.count, second, 1)
            self.pieces = [held, other]
            if not self.tail:
                self.share()
        return self.pieces[0]

    def share(self, *others):
        if self.plain:
            self.pieces += [
                shifted(after(part, *(array for array in others if array is not part)), self.count, self.levels[2], 1)
                for part in self.pieces
            ]


class Scatter:
    def __init__(self, kept, sent, count, rows):
        self.count, self.levels = count, levels_of(count)
        self.plain = is_plain(count, rows)
        if self.plain:
            self.own, self.other = kept, [shifted(part, count, self.levels[2], -1) for part in sent]
            return
        held = jnp.concatenate([jnp.concatenate(side, axis=1) for side in (kept, sent)], axis=0)
        for level in reversed(self.levels):
            size = level[1]
            pieces = held.reshape(size, held.shape[0] // size, held.shape[1])
            total = wide(pieces[0])
            for step in range(1, size):
                total = total + wide(shifted(pieces[step], count, level, -step))
            held = total if level == self.levels[0] else low(total)
        self.other, self.begun, self.parts = [held], held, [held]

    def second(self):
        if self.plain:
            self.own, sent = add_halves(self.own, self.other)
            self.other = [shifted(part, self.count, self.levels[1], -1) for part in sent]

    def third(self):
        if self.plain:
            pieces = add_split(self.own, self.other, 4)
            self.parts = [pieces[0]]
            for step in range(1, 4):
                self.parts.append(shifted(pieces[step], self.count, self.levels[0], -step))
            self.other, self.begun = self.parts[1:], pieces[0]

def placement(count, width):
    device = lax.axis_index("dp")
    place = jnp.arange(count)
    owner, weight = jnp.zeros_like(place), 1
    for stride, size in levels_of(count):
        step = (place // weight) % size
        owner = owner + ((device // stride) % size - step + size) % size * stride
        weight *= size
    rows = width // count
    natural = (owner[:, None] * rows + jnp.arange(rows)[None, :]).reshape(width)
    there = jnp.arange(width)
    return low(natural[None, :] == there[:, None]), low(natural[:, None] == there[None, :])


def spec(block, *place):
    return pl.BlockSpec(block, lambda step: place)


latest = []


def wait_for(*arrays):
    latest.extend(arrays)


def run(body, out_shapes, operands, specs=None, scratch=(), limit=LIMIT, last=False, weight=0):
    if last:
        limit = 60
        specs = [spec(array.shape, *[0] * array.ndim) for array in operands]
    grid = () if specs is None else (1,)
    specs = [None] * len(operands) if specs is None else specs
    specs = [
        pl.BlockSpec(memory_space=pltpu.VMEM) if given is None else given for given in specs
    ]
    count, waits = len(operands), len(latest)

    def ordered(*refs):
        body(*refs[:count], *refs[count + waits :])

    results = pl.pallas_call(
        ordered,
        out_shape=out_shapes,
        grid=grid,
        in_specs=specs + [pl.BlockSpec(memory_space=pl.ANY)] * waits,
        out_specs=[
            spec(shape.shape, *[0] * len(shape.shape)) if last else pl.BlockSpec(memory_space=pltpu.VMEM)
            for shape in out_shapes
        ],
        scratch_shapes=scratch,
        compiler_params=pltpu.CompilerParams(vmem_limit_bytes=limit * 1024 * 1024),
        cost_estimate=pl.CostEstimate(flops=weight, bytes_accessed=0, transcendentals=0),
    )(*operands, *latest)
    latest[:] = [min(results, key=lambda array: array.size)]
    return results


def half(*shape):
    return jax.ShapeDtypeStruct(shape, jnp.bfloat16)


def full(*shape):
    return jax.ShapeDtypeStruct(shape, jnp.float32)


def stack_rows(pieces, parts=1, weight=0):
    rows, width = pieces[0].shape
    rows //= parts

    def body(*refs):
        for number, ref in enumerate(refs[:-parts]):
            for part, out in enumerate(refs[-parts:]):
                out[number * rows : (number + 1) * rows, :] = ref[part * rows : (part + 1) * rows, :]

    stacked = run(body, [half(rows * len(pieces), width)] * parts, pieces, limit=SMALL, weight=weight)
    return stacked if parts > 1 else stacked[0]


def add_halves(left, right):
    rows = left[0].shape[0] // 2

    def body(*refs):
        pieces = len(left)
        for i in range(pieces):
            total = wide(refs[i][...]) + wide(refs[i + pieces][...])
            refs[i + 2 * pieces][...] = low(total[:rows])
            refs[i + 3 * pieces][...] = low(total[rows:])

    shapes = [half(rows, piece.shape[1]) for piece in left]
    results = run(body, shapes * 2, [*left, *right], limit=SMALL)
    return results[: len(left)], results[len(left) :]


def add_split(left, right, parts):
    rows = left[0].shape[0] // parts
    sizes = [piece.shape[1] for piece in left]

    def body(*refs):
        start = 0
        for i, size in enumerate(sizes):
            for number, out in enumerate(refs[2 * len(sizes) :]):
                part = slice(number * rows, (number + 1) * rows)
                total = wide(refs[i][part, :]) + wide(refs[i + len(sizes)][part, :])
                out[:, start : start + size] = low(total)
            start += size

    return run(body, [half(rows, sum(sizes))] * parts, [*left, *right], limit=SMALL)


def total_of(refs):
    total = wide(refs[0][...])
    for ref in refs[1:]:
        total = total + wide(ref[...])
    return total


def add_all(parts):
    def body(*refs):
        refs[-1][...] = total_of(refs[:-1])

    return run(body, [full(*parts[0].shape)], parts, limit=SMALL, weight=WEIGHT)[0]


def gain_columns(total, weights, gains):
    rows, room = total.shape[0], weights.shape[1]

    def body(total_ref, weights_ref, gains_ref, columns_ref):
        share = jnp.sum(wide(weights_ref[...]) * total_ref[:, :room], axis=1, keepdims=True)
        lane = lax.broadcasted_iota(jnp.int32, (rows, 2), 1)
        columns_ref[...] = jnp.where(lane == 0, gains_ref[:, 1:], share / gains_ref[:, :1])

    return run(body, [full(rows, 2)], [total, weights, gains], limit=SMALL)[0]


def finish_feed_forward(total, gains, hidden):
    rows, room = total.shape[0], total.shape[1] // 3

    def body(total_ref, gains_ref, sum_ref, down_ref):
        gain = gains_ref[:, :1]
        down_ref[...] = total_ref[:, 2 * room : 2 * room + hidden]
        sum_ref[:, 0, :] = total_ref[:, :hidden] * gain
        sum_ref[:, 1, :] = total_ref[:, room : room + hidden] * gain

    return run(body, [full(rows, 2, hidden), full(rows, hidden)], [total, gains], last=True)


def finish_attention(parts, query_keys, values_out, columns):
    rows, inner = values_out.shape[0], values_out.shape[1] // 2

    def body(*refs):
        *parts, query_keys_ref, values_out_ref, columns_ref, sum_ref, out_ref, share_ref = refs
        total, gain = total_of(parts), columns_ref[:, :1]
        for number in range(3):
            sum_ref[number] = total[:, number * inner : (number + 1) * inner] * gain
        out_ref[...] = total[:, 3 * inner :]
        share = jnp.sum(wide(query_keys_ref[...]) * total[:, : 2 * inner], axis=1, keepdims=True)
        values = wide(values_out_ref[:, :inner]) * total[:, 2 * inner : 3 * inner]
        share = (share + jnp.sum(values, axis=1, keepdims=True)) / gain
        place = lax.broadcasted_iota(jnp.int32, (rows, rows), 0) == lax.broadcasted_iota(jnp.int32, (rows, rows), 1)
        for number, column in enumerate((share, columns_ref[:, 1:])):
            spread = jnp.where(place, column, jnp.zeros((rows, rows), jnp.float32))
            share_ref[number : number + 1, :] = jnp.sum(spread, axis=0, keepdims=True)

    return run(
        body,
        [full(3, rows, inner), full(rows, inner), full(2, rows)],
        [*parts, query_keys, values_out, columns],
        last=True,
    )


def normalize(values):
    average = jnp.mean(values, axis=-1, keepdims=True)
    centered = values - average
    variance = jnp.mean(centered * centered, axis=-1, keepdims=True)
    inverse = lax.rsqrt(variance + EPSILON)
    return centered * inverse, inverse


def norm_back(scaled, normed, inverse):
    first = jnp.mean(scaled, axis=-1, keepdims=True)
    second = jnp.mean(scaled * normed, axis=-1, keepdims=True)
    return inverse * (scaled - first - normed * second)


def partner(values):
    lane = lax.broadcasted_iota(jnp.int32, values.shape, 1)
    return jnp.where(
        lane % HD < HD // 2,
        pltpu.roll(values, LANES - HD // 2, 1),
        pltpu.roll(values, HD // 2, 1),
    )


def group(number):
    return slice(number * LANES, (number + 1) * LANES)


def rows_of(refs):
    return jnp.concatenate([ref[...] for ref in refs], axis=0)


def both_heads(values):
    lane = lax.broadcasted_iota(jnp.int32, values.shape, 1)
    nothing = jnp.zeros_like(values)
    return jnp.concatenate(
        [jnp.where(lane < HD, values, nothing), jnp.where(lane < HD, nothing, values)], axis=0
    )


def one_pair(values):
    rows = values.shape[0] // 2
    lane = lax.broadcasted_iota(jnp.int32, (rows, values.shape[1]), 1)
    return jnp.where(lane < HD, values[:rows], values[rows:])


def tiles_of(count, inner):
    for block in range(count // BLOCK):
        start = min(max(block * BLOCK - HALF, 0), count - WINDOW)
        for pair in range(inner // LANES):
            number = block * (inner // LANES) + pair
            yield number, pair, slice(block * BLOCK, (block + 1) * BLOCK), slice(start, start + WINDOW)


def prepare(tokens, order):
    def body(tokens_ref, order_ref, inputs_ref, normed_ref):
        inputs = product(tokens_ref[...], order_ref[...])
        inputs_ref[...] = low(inputs)
        normed_ref[...] = low(normalize(inputs)[0])

    return run(body, [half(*tokens.shape)] * 2, [tokens, order])


def reorder(values, order):
    def body(values_ref, order_ref, out_ref):
        out_ref[...] = low(product(values_ref[...], order_ref[...]))

    return run(body, [half(*values.shape)], [values, order])[0]


def attend_shares(normed, pieces, cosine, sine, column, row):
    count, width = normed.shape
    inner = pieces[0].shape[1] // 2
    tiles = list(tiles_of(count, inner))

    def body(normed_ref, a, b, c, d, cosine_ref, sine_ref, column_ref, row_ref, query_ref, keys_ref, shares_ref):
        projected = product(normed_ref[...], rows_of((a, b, c, d)))
        cosine, sine = cosine_ref[...], sine_ref[...]
        for number in range(inner // LANES):
            part = projected[:, group(number)]
            query_ref[:, group(number)] = low(part * cosine + partner(part) * sine)
            part = projected[:, group(number + inner // LANES)]
            keys_ref[:, group(number)] = low(part * cosine + partner(part) * sine)
        for number, pair, queries, window in tiles:
            if pair == 0:
                near = lax.broadcasted_iota(jnp.int32, (WINDOW, BLOCK), 0) + window.start
                near = near - lax.broadcasted_iota(jnp.int32, (WINDOW, BLOCK), 1) - queries.start
                allowed = (jnp.abs(near) <= HALF) & (column_ref[window, :] == row_ref[:, queries])
                allowed = jnp.concatenate([allowed.astype(jnp.float32)] * 2, axis=1) > 0.5
            query = both_heads(query_ref[queries, group(pair)])
            scores = product(keys_ref[window, group(pair)], query, NT) * SCALE
            scores = jnp.where(allowed, scores, MASKED)
            powers = jnp.exp(scores - jnp.max(scores, axis=0, keepdims=True))
            total = jnp.sum(powers, axis=0, keepdims=True)
            shares_ref[number] = low(powers * (1.0 / total))

    return run(
        body,
        [half(count, inner), half(count, inner), half(len(tiles), WINDOW, 2 * BLOCK)],
        [normed, *pieces, cosine, sine, column, row],
    )


def attend_values(normed, pieces, shares):
    count, width = normed.shape
    inner = pieces[0].shape[1] // 2
    tiles = list(tiles_of(count, inner))

    def body(normed_ref, a, b, c, d, shares_ref, values_ref, context_ref, out_ref):
        matrix = rows_of((a, b, c, d))
        values_ref[...] = low(product(normed_ref[...], matrix[:, :inner]))
        for number, pair, queries, window in tiles:
            both = product(shares_ref[number], values_ref[window, group(pair)], TN)
            context_ref[queries, group(pair)] = low(one_pair(both))
        out_ref[...] = low(product(context_ref[...], matrix[:, inner:], NT))

    return run(
        body,
        [half(count, inner), half(count, inner), half(count, width)],
        [normed, *pieces, shares],
    )


def settle(inputs, own, other):
    def body(inputs_ref, own_ref, other_ref, middle_ref, normed_ref):
        middle = wide(inputs_ref[...]) + (wide(own_ref[...]) + wide(other_ref[...]))
        middle_ref[...] = middle
        normed_ref[...] = low(normalize(middle)[0])

    return run(body, [full(*inputs.shape), half(*inputs.shape)], [inputs, own, other], weight=WEIGHT)


def feed_forward(normed, upstream, gates_in, down):
    count, width = normed.shape
    hidden = down[0].shape[1]

    def body(normed_ref, upstream_ref, a, b, c, d, e, f, g, h,
             mixed_ref, gates_ref, forward_ref, back_ref):
        matrix, down = rows_of((a, b, c, d)), rows_of((e, f, g, h))
        gates = product(normed_ref[...], matrix)
        active, factor = gates[:, :hidden], gates[:, hidden:]
        chance = 0.5 + 0.5 * lax.erf(active * 0.7071067811865476)
        bent = active * chance
        mixed = low(bent * factor)
        mixed_ref[...] = mixed
        forward_ref[...] = low(product(mixed, down, NT))
        grad_mixed = product(upstream_ref[...], down)
        slope = chance + active * (0.3989422804014327 * jnp.exp(-0.5 * active * active))
        gates_ref[:, :hidden] = low(grad_mixed * factor * slope)
        gates_ref[:, hidden:] = low(grad_mixed * bent)
        back_ref[...] = low(product(gates_ref[...], matrix, NT))

    return run(
        body,
        [half(count, hidden), half(count, 2 * hidden), half(count, width), half(count, width)],
        [normed, upstream, *gates_in, *down],
    )


def feed_forward_grads(normed, mixed, gates, upstream):
    count, width = upstream.shape
    hidden = mixed.shape[1]

    def body(normed_ref, mixed_ref, gates_ref, upstream_ref, *outs):
        for number in range(2):
            part = slice(number * width // 2, (number + 1) * width // 2)
            active_ref, factor_ref, down_ref = outs[3 * number : 3 * number + 3]
            both = product(normed_ref[:, part], gates_ref[...], TN)
            active_ref[...] = low(both[:, :hidden])
            factor_ref[...] = low(both[:, hidden:])
            down_ref[...] = low(product(upstream_ref[:, part], mixed_ref[...], TN))

    return run(body, [half(width // 2, hidden)] * 6, [normed, mixed, gates, upstream])


def add_output(middle, own, others, order):
    cut = others[0].shape[0]

    def body(middle_ref, own_ref, upper_ref, lower_ref, order_ref, out_ref):
        for part, ref in ((slice(0, cut), upper_ref), (slice(cut, None), lower_ref)):
            total = low(middle_ref[part, :] + (wide(own_ref[part, :]) + wide(ref[...])))
            out_ref[part, :] = low(product(total, order_ref[...]))

    return run(body, [half(*middle.shape)], [middle, own, *others, order])[0]


def attend_back_values(upstream, middle, own, other, pieces, context, shares):
    count, width = upstream.shape
    inner = context.shape[1]
    tiles = list(tiles_of(count, inner))

    def body(upstream_ref, middle_ref, own_ref, other_ref, a, b, c, d, context_ref, shares_ref,
             branch_ref, grad_context_ref, grad_values_ref, total_ref):
        matrix = rows_of((a, b, c, d))
        normed, inverse = normalize(middle_ref[...])
        scaled = wide(own_ref[...]) + wide(other_ref[...])
        grad_middle = wide(upstream_ref[...]) + norm_back(scaled, normed, inverse)
        branch_ref[...] = low(grad_middle)
        grad_context_ref[...] = low(product(branch_ref[...], matrix))
        total_ref[...] = jnp.zeros_like(total_ref)
        for number, pair, queries, window in tiles:
            upper = both_heads(grad_context_ref[queries, group(pair)])
            total_ref[window, group(pair)] += product(shares_ref[number], upper)
        grad_values_ref[...] = low(total_ref[...])

    return run(
        body,
        [half(count, width), half(count, inner), half(count, inner)],
        [upstream, middle, own, other, *pieces, context, shares],
        [None] * 4 + [spec((width // PIECES, inner), 0, 1)] * PIECES + [None] * 2,
        scratch=[pltpu.VMEM((count, inner), jnp.float32)],
    )


def attend_back_shares(query, keys, values, grad_context, shares, grad_values, cosine, sine, query_keys, values_out):
    count, inner = query.shape
    width = query_keys[0].shape[0] * PIECES
    tiles = list(tiles_of(count, inner))

    def body(query_ref, keys_ref, values_ref, grad_context_ref, shares_ref, grad_values_ref, cosine_ref, sine_ref,
             a, b, c, d, e, f, g, h, grad_ref, back_ref, total_ref):
        total_ref[...] = jnp.zeros_like(total_ref)
        cosine, sine = cosine_ref[...], sine_ref[...]
        for number, pair, queries, window in tiles:
            upper = both_heads(grad_context_ref[queries, group(pair)])
            grad_shares = product(values_ref[window, group(pair)], upper, NT)
            shares = wide(shares_ref[number])
            sums = jnp.sum(shares * grad_shares, axis=0, keepdims=True)
            grad_scores = low(shares * (grad_shares - sums))
            grad_query = one_pair(product(grad_scores, keys_ref[window, group(pair)], TN)) * SCALE
            grad_query = grad_query * cosine[queries] - partner(grad_query) * sine[queries]
            grad_ref[queries, group(pair)] = low(grad_query)
            lower = both_heads(query_ref[queries, group(pair)])
            total_ref[window, group(pair)] += product(grad_scores, lower)
        for pair in range(inner // LANES):
            grad_keys = total_ref[:, group(pair)] * SCALE
            grad_keys = grad_keys * cosine - partner(grad_keys) * sine
            grad_ref[:, group(pair + inner // LANES)] = low(grad_keys)
        back = product(grad_ref[...], rows_of((a, b, c, d)), NT)
        back_ref[...] = low(back + product(grad_values_ref[...], rows_of((e, f, g, h)), NT))

    return run(
        body,
        [half(count, 2 * inner), half(count, width)],
        [query, keys, values, grad_context, shares, grad_values, cosine, sine, *query_keys, *values_out],
        [None] * (8 + PIECES) + [spec((width // PIECES, inner), 0, 0)] * PIECES,
        scratch=[pltpu.VMEM((count, inner), jnp.float32)],
    )


def paired_grads(groups):
    pairs = [pair for group in groups for pair in group]
    count, width = pairs[0][0].shape
    sizes = [sum(right.shape[1] for _, right in group) for group in groups]

    def body(*refs):
        outs, number = refs[2 * len(pairs) :], 0
        for i, group in enumerate(groups):
            start = 0
            for _, right in group:
                size = right.shape[1]
                for side in range(2):
                    part = slice(side * width // 2, (side + 1) * width // 2)
                    both = product(refs[2 * number][:, part], refs[2 * number + 1][...], TN)
                    outs[2 * i + side][:, start : start + size] = low(both)
                start += size
                number += 1

    return run(
        body,
        [half(width // 2, size) for size in sizes for _ in range(2)],
        [array for pair in pairs for array in pair],
    )


def input_grads(branch, inputs, own, other, order):
    count, width = inputs.shape

    def body(branch_ref, inputs_ref, own_ref, other_ref, order_ref, out_ref):
        normed, inverse = normalize(wide(inputs_ref[...]))
        scaled = wide(own_ref[...]) + wide(other_ref[...])
        total = wide(branch_ref[...]) + norm_back(scaled, normed, inverse)
        out_ref[...] = product(low(total), order_ref[...])

    return run(
        body,
        [full(count, width)],
        [branch, inputs, own, other, order],
        last=True,
    )[0]


def rope_tables(positions):
    frequency = THETA ** (-jnp.arange(0, HD, 2).astype(jnp.float32) / HD)
    angle = positions.astype(jnp.float32)[:, None] * jnp.tile(frequency, LANES // (HD // 2))[None, :]
    sign = jnp.where(jnp.arange(LANES) % HD < HD // 2, -1.0, 1.0)
    return jnp.cos(angle), jnp.sin(angle) * sign[None, :]


def padded(values, width):
    return jnp.pad(values, ((0, 0), (0, width - values.shape[1])))


def per_device(
    devices, tokens, seg_ids, positions, gain_attn, w_qkv, w_attn_out, gain_mlp, w_in, w_mlp_out, cotangent
):
    width = tokens.shape[1]
    rows, _, inner = w_qkv.shape
    hidden = w_in.shape[2]
    room = -(-hidden // LANES) * LANES
    gain_one, gain_two = wide(gain_attn)[:, None], wide(gain_mlp)[:, None]
    scaled_qkv = [low(wide(w_qkv[:, i]) * gain_one) for i in range(3)]
    scaled_in = [padded(low(wide(w_in[:, i]) * gain_two), room) for i in range(2)]
    shard_one = jnp.concatenate(scaled_qkv[:2], axis=1)
    shard_two = jnp.concatenate([scaled_qkv[2], w_attn_out.T], axis=1)
    shard_three = jnp.concatenate(scaled_in, axis=1)
    shard_four = padded(w_mlp_out.T, room)
    latest.clear()
    query_keys = Gather(shard_one, devices)
    down = Gather(shard_four, devices, late=True)
    order, back = placement(devices, width)
    cosine, sine = rope_tables(positions)
    column, row = seg_ids[:, None], seg_ids[None, :]
    held = query_keys.stack()
    values_out = Gather(after(shard_two, held), devices)
    inputs, normed_one = prepare(tokens, order)
    wait_for(query_keys.other, query_keys.pieces[2])
    held = values_out.stack()
    gates_in = Gather(after(shard_three, held), devices, tail=True)
    wait_for(cosine, sine, column)
    down.join_rows()
    query, keys, shares = attend_shares(normed_one, query_keys.pieces, cosine, sine, column, row)
    wait_for(values_out.other)
    held = gates_in.stack(WEIGHT)
    down.begin(held)
    values, context, own = attend_values(normed_one, values_out.pieces, shares)
    other = swapped(own)
    gains = jnp.concatenate([gain_two, gain_one], axis=1)

    upstream = reorder(cotangent, order)
    down.stack()
    gates_in.share(gates_in.other)
    middle, normed_two = settle(inputs, own, other)
    mixed, grad_gates, own_out, own_two = feed_forward(
        normed_two, upstream, gates_in.pieces, down.pieces
    )
    other_two = swapped(own_two)
    grads_mlp = feed_forward_grads(normed_two, mixed, grad_gates, upstream)
    sums_mlp = Scatter(grads_mlp[:3], grads_mlp[3:], devices, rows)
    sums_mlp.second()
    early = own_out.shape[0] // EARLY
    upper_out = swapped(own_out[:early])
    branch, grad_context, grad_values = attend_back_values(
        upstream, middle, own_two, other_two, values_out.pieces, context, shares
    )
    grad_query_keys, own_one = attend_back_shares(
        query, keys, values, grad_context, shares, grad_values, cosine, sine, query_keys.pieces, values_out.pieces
    )
    other_one = swapped(own_one)
    wait_for(upper_out, *sums_mlp.other)
    kept, sent = paired_grads(
        [[(normed_one, grad_query_keys), (normed_one, grad_values), (branch, context)]]
    )
    sums = Scatter([kept], [sent], devices, rows)
    sums_mlp.third()
    sums.second()
    sum_mlp = add_all(sums_mlp.parts)
    sums.third()
    lower_out = swapped(after(own_out[early:], sums.begun))
    columns = gain_columns(sum_mlp, shard_three, gains)
    grad_input = input_grads(branch, inputs, own_one, other_one, back)
    output = add_output(middle, own_out, (upper_out, lower_out), back)
    sum_qkv, sum_out, share = finish_attention(sums.parts, shard_one, shard_two, columns)
    sum_in, sum_down = finish_feed_forward(sum_mlp, gains, hidden)
    gains = after(share, sum_down) + swapped(share)
    sum_qkv = jnp.transpose(sum_qkv, (1, 0, 2))
    return (output, grad_input, gains[0], sum_qkv, sum_out.T, gains[1], sum_in, sum_down.T)


def solution(mesh):
    return jax.shard_map(
        functools.partial(per_device, mesh.shape["dp"]),
        mesh=mesh,
        in_specs=(
            P("dp", None),
            P("dp"),
            P("dp"),
            P("dp"),
            P("dp", None, "tensor"),
            P("tensor", "dp"),
            P("dp"),
            P("dp", None, "tensor"),
            P("tensor", "dp"),
            P("dp", None),
        ),
        out_specs=(
            P("dp", None),
            P("dp", None),
            P("dp"),
            P("dp", None, "tensor"),
            P("tensor", "dp"),
            P("dp"),
            P("dp", None, "tensor"),
            P("tensor", "dp"),
        ),
        check_vma=False,
    )
```

```python
import functools

import jax
import jax.numpy as jnp
from jax import lax
from jax.experimental import pallas as pl
from jax.experimental.pallas import tpu as pltpu
from jax.sharding import PartitionSpec as P

HD = 64
HALF = 64
LIMIT = 16
SMALL = 4
LANES = 128
BLOCK = 128
WINDOW = 256
EARLY = 2
WEIGHT = 10**10
PIECES = 4

EPSILON = 1e-05
THETA = 10000.0
MASKED = -1e30
SCALE = HD ** (-0.5)

NN = (((1,), (0,)), ((), ()))
NT = (((1,), (1,)), ((), ()))
TN = (((0,), (0,)), ((), ()))


def product(left, right, dims=NN):
    return lax.dot_general(left, right, dims, preferred_element_type=jnp.float32)


def low(values):
    return values.astype(jnp.bfloat16)


def wide(values):
    return values.astype(jnp.float32)


def levels_of(count):
    levels, stride = [], count
    while stride > 1:
        size = 4 if stride % 8 == 0 else 2 if stride % 2 == 0 else stride
        stride //= size
        levels.append((stride, size))
    return levels


def shifted(values, count, level, step):
    stride, size = level
    pairs = []
    for device in range(count):
        digit = (device // stride) % size
        pairs.append((device, device + ((digit + step) % size - digit) * stride))
    return lax.ppermute(values, "dp", pairs)


def swapped(values):
    return lax.ppermute(values, "tensor", [(0, 1), (1, 0)])


def is_plain(count, rows):
    return levels_of(count) == [(4, 4), (2, 2), (1, 2)] and rows % 16 == 0


def after(values, *others):
    return lax.optimization_barrier((values, *others))[0]


class Gather:
    def __init__(self, shard, count, late=False, tail=False):
        self.count, self.levels, self.late, self.tail = count, levels_of(count), late, tail
        self.plain = is_plain(count, shard.shape[0])
        self.shard = shard
        if not self.plain:
            held = shard
            for level in self.levels:
                held = jnp.concatenate(
                    [held] + [shifted(held, count, level, step) for step in range(1, level[1])], axis=0
                )
            self.pieces = jnp.split(held, PIECES, axis=0)
            self.other = self.pieces[0]
        elif late:
            self.other = shifted(shard, count, self.levels[1], 1)
        else:
            self.received = self.along_first(shard)

    def along_first(self, rows):
        return [shifted(rows, self.count, self.levels[0], step) for step in range(1, 4)]

    def join_rows(self):
        if self.plain:
            self.shard = stack_rows([self.shard, self.other])

    def begin(self, other):
        if self.plain:
            self.shard = after(self.shard, other)
            self.received = self.along_first(self.shard)

    def stack(self, weight=0):
        if self.plain:
            _, second, third = self.levels
            if self.late:
                held, other = stack_rows([self.shard] + self.received, 2, weight)
            else:
                held = stack_rows([self.shard] + self.received, weight=weight)
                other = self.other = shifted(held, self.count, second, 1)
            self.pieces = [held, other]
            if not self.tail:
                self.share()
        return self.pieces[0]

    def share(self, *others):
        if self.plain:
            self.pieces += [
                shifted(after(part, *(array for array in others if array is not part)), self.count, self.levels[2], 1)
                for part in self.pieces
            ]


class Scatter:
    def __init__(self, kept, sent, count, rows):
        self.count, self.levels = count, levels_of(count)
        self.plain = is_plain(count, rows)
        if self.plain:
            self.own, self.other = kept, [shifted(part, count, self.levels[2], -1) for part in sent]
            return
        held = jnp.concatenate([jnp.concatenate(side, axis=1) for side in (kept, sent)], axis=0)
        for level in reversed(self.levels):
            size = level[1]
            pieces = held.reshape(size, held.shape[0] // size, held.shape[1])
            total = wide(pieces[0])
            for step in range(1, size):
                total = total + wide(shifted(pieces[step], count, level, -step))
            held = total if level == self.levels[0] else low(total)
        self.other, self.begun, self.parts = [held], held, [held]

    def second(self):
        if self.plain:
            self.own, sent = add_halves(self.own, self.other)
            self.other = [shifted(part, self.count, self.levels[1], -1) for part in sent]

    def third(self):
        if self.plain:
            pieces = add_split(self.own, self.other, 4)
            self.parts = [pieces[0]]
            for step in range(1, 4):
                self.parts.append(shifted(pieces[step], self.count, self.levels[0], -step))
            self.other, self.begun = self.parts[1:], pieces[0]

def placement(count, width):
    device = lax.axis_index("dp")
    place = jnp.arange(count)
    owner, weight = jnp.zeros_like(place), 1
    for stride, size in levels_of(count):
        step = (place // weight) % size
        owner = owner + ((device // stride) % size - step + size) % size * stride
        weight *= size
    rows = width // count
    natural = (owner[:, None] * rows + jnp.arange(rows)[None, :]).reshape(width)
    there = jnp.arange(width)
    return low(natural[None, :] == there[:, None]), low(natural[:, None] == there[None, :])


def spec(block, *place):
    return pl.BlockSpec(block, lambda step: place)


latest = []


def wait_for(*arrays):
    latest.extend(arrays)


def run(body, out_shapes, operands, specs=None, scratch=(), limit=LIMIT, last=False, weight=0):
    if last:
        limit = 60
        specs = [spec(array.shape, *[0] * array.ndim) for array in operands]
    grid = () if specs is None else (1,)
    specs = [None] * len(operands) if specs is None else specs
    specs = [
        pl.BlockSpec(memory_space=pltpu.VMEM) if given is None else given for given in specs
    ]
    count, waits = len(operands), len(latest)

    def ordered(*refs):
        body(*refs[:count], *refs[count + waits :])

    results = pl.pallas_call(
        ordered,
        out_shape=out_shapes,
        grid=grid,
        in_specs=specs + [pl.BlockSpec(memory_space=pl.ANY)] * waits,
        out_specs=[
            spec(shape.shape, *[0] * len(shape.shape)) if last else pl.BlockSpec(memory_space=pltpu.VMEM)
            for shape in out_shapes
        ],
        scratch_shapes=scratch,
        compiler_params=pltpu.CompilerParams(vmem_limit_bytes=limit * 1024 * 1024),
        cost_estimate=pl.CostEstimate(flops=weight, bytes_accessed=0, transcendentals=0),
    )(*operands, *latest)
    latest[:] = [min(results, key=lambda array: array.size)]
    return results


def half(*shape):
    return jax.ShapeDtypeStruct(shape, jnp.bfloat16)


def full(*shape):
    return jax.ShapeDtypeStruct(shape, jnp.float32)


def stack_rows(pieces, parts=1, weight=0):
    rows, width = pieces[0].shape
    rows //= parts

    def body(*refs):
        for number, ref in enumerate(refs[:-parts]):
            for part, out in enumerate(refs[-parts:]):
                out[number * rows : (number + 1) * rows, :] = ref[part * rows : (part + 1) * rows, :]

    stacked = run(body, [half(rows * len(pieces), width)] * parts, pieces, limit=SMALL, weight=weight)
    return stacked if parts > 1 else stacked[0]


def add_halves(left, right):
    rows = left[0].shape[0] // 2

    def body(*refs):
        pieces = len(left)
        for i in range(pieces):
            total = wide(refs[i][...]) + wide(refs[i + pieces][...])
            refs[i + 2 * pieces][...] = low(total[:rows])
            refs[i + 3 * pieces][...] = low(total[rows:])

    shapes = [half(rows, piece.shape[1]) for piece in left]
    results = run(body, shapes * 2, [*left, *right], limit=SMALL)
    return results[: len(left)], results[len(left) :]


def add_split(left, right, parts):
    rows = left[0].shape[0] // parts
    sizes = [piece.shape[1] for piece in left]

    def body(*refs):
        start = 0
        for i, size in enumerate(sizes):
            for number, out in enumerate(refs[2 * len(sizes) :]):
                part = slice(number * rows, (number + 1) * rows)
                total = wide(refs[i][part, :]) + wide(refs[i + len(sizes)][part, :])
                out[:, start : start + size] = low(total)
            start += size

    return run(body, [half(rows, sum(sizes))] * parts, [*left, *right], limit=SMALL)


def total_of(refs):
    total = wide(refs[0][...])
    for ref in refs[1:]:
        total = total + wide(ref[...])
    return total


def add_all(parts):
    def body(*refs):
        refs[-1][...] = total_of(refs[:-1])

    return run(body, [full(*parts[0].shape)], parts, limit=SMALL, weight=WEIGHT)[0]


def gain_columns(total, weights, gains):
    rows, room = total.shape[0], weights.shape[1]

    def body(total_ref, weights_ref, gains_ref, columns_ref):
        share = jnp.sum(wide(weights_ref[...]) * total_ref[:, :room], axis=1, keepdims=True)
        lane = lax.broadcasted_iota(jnp.int32, (rows, 2), 1)
        columns_ref[...] = jnp.where(lane == 0, gains_ref[:, 1:], share / gains_ref[:, :1])

    return run(body, [full(rows, 2)], [total, weights, gains], limit=SMALL)[0]


def finish_feed_forward(total, gains, hidden):
    rows, room = total.shape[0], total.shape[1] // 3

    def body(total_ref, gains_ref, sum_ref, down_ref):
        gain = gains_ref[:, :1]
        down_ref[...] = total_ref[:, 2 * room : 2 * room + hidden]
        sum_ref[:, 0, :] = total_ref[:, :hidden] * gain
        sum_ref[:, 1, :] = total_ref[:, room : room + hidden] * gain

    return run(body, [full(rows, 2, hidden), full(rows, hidden)], [total, gains], last=True)


def finish_attention(parts, query_keys, values_out, columns):
    rows, inner = values_out.shape[0], values_out.shape[1] // 2

    def body(*refs):
        *parts, query_keys_ref, values_out_ref, columns_ref, sum_ref, out_ref, share_ref = refs
        total, gain = total_of(parts), columns_ref[:, :1]
        for number in range(3):
            sum_ref[number] = total[:, number * inner : (number + 1) * inner] * gain
        out_ref[...] = total[:, 3 * inner :]
        share = jnp.sum(wide(query_keys_ref[...]) * total[:, : 2 * inner], axis=1, keepdims=True)
        values = wide(values_out_ref[:, :inner]) * total[:, 2 * inner : 3 * inner]
        share = (share + jnp.sum(values, axis=1, keepdims=True)) / gain
        place = lax.broadcasted_iota(jnp.int32, (rows, rows), 0) == lax.broadcasted_iota(jnp.int32, (rows, rows), 1)
        for number, column in enumerate((share, columns_ref[:, 1:])):
            spread = jnp.where(place, column, jnp.zeros((rows, rows), jnp.float32))
            share_ref[number : number + 1, :] = jnp.sum(spread, axis=0, keepdims=True)

    return run(
        body,
        [full(3, rows, inner), full(rows, inner), full(2, rows)],
        [*parts, query_keys, values_out, columns],
        last=True,
    )


def normalize(values):
    average = jnp.mean(values, axis=-1, keepdims=True)
    centered = values - average
    variance = jnp.mean(centered * centered, axis=-1, keepdims=True)
    inverse = lax.rsqrt(variance + EPSILON)
    return centered * inverse, inverse


def norm_back(scaled, normed, inverse):
    first = jnp.mean(scaled, axis=-1, keepdims=True)
    second = jnp.mean(scaled * normed, axis=-1, keepdims=True)
    return inverse * (scaled - first - normed * second)


def partner(values):
    lane = lax.broadcasted_iota(jnp.int32, values.shape, 1)
    return jnp.where(
        lane % HD < HD // 2,
        pltpu.roll(values, LANES - HD // 2, 1),
        pltpu.roll(values, HD // 2, 1),
    )


def group(number):
    return slice(number * LANES, (number + 1) * LANES)


def rows_of(refs):
    return jnp.concatenate([ref[...] for ref in refs], axis=0)


def both_heads(values):
    lane = lax.broadcasted_iota(jnp.int32, values.shape, 1)
    nothing = jnp.zeros_like(values)
    return jnp.concatenate(
        [jnp.where(lane < HD, values, nothing), jnp.where(lane < HD, nothing, values)], axis=0
    )


def one_pair(values):
    rows = values.shape[0] // 2
    lane = lax.broadcasted_iota(jnp.int32, (rows, values.shape[1]), 1)
    return jnp.where(lane < HD, values[:rows], values[rows:])


def tiles_of(count, inner):
    for block in range(count // BLOCK):
        start = min(max(block * BLOCK - HALF, 0), count - WINDOW)
        for pair in range(inner // LANES):
            number = block * (inner // LANES) + pair
            yield number, pair, slice(block * BLOCK, (block + 1) * BLOCK), slice(start, start + WINDOW)


def prepare(tokens, order):
    def body(tokens_ref, order_ref, inputs_ref, normed_ref):
        inputs = product(tokens_ref[...], order_ref[...])
        inputs_ref[...] = low(inputs)
        normed_ref[...] = low(normalize(inputs)[0])

    return run(body, [half(*tokens.shape)] * 2, [tokens, order])


def reorder(values, order):
    def body(values_ref, order_ref, out_ref):
        out_ref[...] = low(product(values_ref[...], order_ref[...]))

    return run(body, [half(*values.shape)], [values, order])[0]


def attend_shares(normed, pieces, cosine, sine, column, row):
    count, width = normed.shape
    inner = pieces[0].shape[1] // 2
    tiles = list(tiles_of(count, inner))

    def body(normed_ref, a, b, c, d, cosine_ref, sine_ref, column_ref, row_ref, query_ref, keys_ref, shares_ref):
        projected = product(normed_ref[...], rows_of((a, b, c, d)))
        cosine, sine = cosine_ref[...], sine_ref[...]
        for number in range(inner // LANES):
            part = projected[:, group(number)]
            query_ref[:, group(number)] = low(part * cosine + partner(part) * sine)
            part = projected[:, group(number + inner // LANES)]
            keys_ref[:, group(number)] = low(part * cosine + partner(part) * sine)
        for number, pair, queries, window in tiles:
            if pair == 0:
                near = lax.broadcasted_iota(jnp.int32, (WINDOW, BLOCK), 0) + window.start
                near = near - lax.broadcasted_iota(jnp.int32, (WINDOW, BLOCK), 1) - queries.start
                allowed = (jnp.abs(near) <= HALF) & (column_ref[window, :] == row_ref[:, queries])
                allowed = jnp.concatenate([allowed.astype(jnp.float32)] * 2, axis=1) > 0.5
            query = both_heads(query_ref[queries, group(pair)])
            scores = product(keys_ref[window, group(pair)], query, NT) * SCALE
            scores = jnp.where(allowed, scores, MASKED)
            powers = jnp.exp(scores - jnp.max(scores, axis=0, keepdims=True))
            total = jnp.sum(powers, axis=0, keepdims=True)
            shares_ref[number] = low(powers * (1.0 / total))

    return run(
        body,
        [half(count, inner), half(count, inner), half(len(tiles), WINDOW, 2 * BLOCK)],
        [normed, *pieces, cosine, sine, column, row],
    )


def attend_values(normed, pieces, shares):
    count, width = normed.shape
    inner = pieces[0].shape[1] // 2
    tiles = list(tiles_of(count, inner))

    def body(normed_ref, a, b, c, d, shares_ref, values_ref, context_ref, out_ref):
        matrix = rows_of((a, b, c, d))
        values_ref[...] = low(product(normed_ref[...], matrix[:, :inner]))
        for number, pair, queries, window in tiles:
            both = product(shares_ref[number], values_ref[window, group(pair)], TN)
            context_ref[queries, group(pair)] = low(one_pair(both))
        out_ref[...] = low(product(context_ref[...], matrix[:, inner:], NT))

    return run(
        body,
        [half(count, inner), half(count, inner), half(count, width)],
        [normed, *pieces, shares],
    )


def settle(inputs, own, other):
    def body(inputs_ref, own_ref, other_ref, middle_ref, normed_ref):
        middle = wide(inputs_ref[...]) + (wide(own_ref[...]) + wide(other_ref[...]))
        middle_ref[...] = middle
        normed_ref[...] = low(normalize(middle)[0])

    return run(body, [full(*inputs.shape), half(*inputs.shape)], [inputs, own, other], weight=WEIGHT)


def feed_forward(normed, upstream, gates_in, down):
    count, width = normed.shape
    hidden = down[0].shape[1]

    def body(normed_ref, upstream_ref, a, b, c, d, e, f, g, h,
             mixed_ref, gates_ref, forward_ref, back_ref):
        matrix, down = rows_of((a, b, c, d)), rows_of((e, f, g, h))
        gates = product(normed_ref[...], matrix)
        active, factor = gates[:, :hidden], gates[:, hidden:]
        chance = 0.5 + 0.5 * lax.erf(active * 0.7071067811865476)
        bent = active * chance
        mixed = low(bent * factor)
        mixed_ref[...] = mixed
        forward_ref[...] = low(product(mixed, down, NT))
        grad_mixed = product(upstream_ref[...], down)
        slope = chance + active * (0.3989422804014327 * jnp.exp(-0.5 * active * active))
        gates_ref[:, :hidden] = low(grad_mixed * factor * slope)
        gates_ref[:, hidden:] = low(grad_mixed * bent)
        back_ref[...] = low(product(gates_ref[...], matrix, NT))

    return run(
        body,
        [half(count, hidden), half(count, 2 * hidden), half(count, width), half(count, width)],
        [normed, upstream, *gates_in, *down],
    )


def feed_forward_grads(normed, mixed, gates, upstream):
    count, width = upstream.shape
    hidden = mixed.shape[1]

    def body(normed_ref, mixed_ref, gates_ref, upstream_ref, *outs):
        for number in range(2):
            part = slice(number * width // 2, (number + 1) * width // 2)
            active_ref, factor_ref, down_ref = outs[3 * number : 3 * number + 3]
            both = product(normed_ref[:, part], gates_ref[...], TN)
            active_ref[...] = low(both[:, :hidden])
            factor_ref[...] = low(both[:, hidden:])
            down_ref[...] = low(product(upstream_ref[:, part], mixed_ref[...], TN))

    return run(body, [half(width // 2, hidden)] * 6, [normed, mixed, gates, upstream])


def add_output(middle, own, others, order):
    cut = others[0].shape[0]

    def body(middle_ref, own_ref, upper_ref, lower_ref, order_ref, out_ref):
        for part, ref in ((slice(0, cut), upper_ref), (slice(cut, None), lower_ref)):
            total = low(middle_ref[part, :] + (wide(own_ref[part, :]) + wide(ref[...])))
            out_ref[part, :] = low(product(total, order_ref[...]))

    return run(body, [half(*middle.shape)], [middle, own, *others, order])[0]


def attend_back_values(upstream, middle, own, other, pieces, context, shares):
    count, width = upstream.shape
    inner = context.shape[1]
    tiles = list(tiles_of(count, inner))

    def body(upstream_ref, middle_ref, own_ref, other_ref, a, b, c, d, context_ref, shares_ref,
             branch_ref, grad_context_ref, grad_values_ref, total_ref):
        matrix = rows_of((a, b, c, d))
        normed, inverse = normalize(middle_ref[...])
        scaled = wide(own_ref[...]) + wide(other_ref[...])
        grad_middle = wide(upstream_ref[...]) + norm_back(scaled, normed, inverse)
        branch_ref[...] = low(grad_middle)
        grad_context_ref[...] = low(product(branch_ref[...], matrix))
        total_ref[...] = jnp.zeros_like(total_ref)
        for number, pair, queries, window in tiles:
            upper = both_heads(grad_context_ref[queries, group(pair)])
            total_ref[window, group(pair)] += product(shares_ref[number], upper)
        grad_values_ref[...] = low(total_ref[...])

    return run(
        body,
        [half(count, width), half(count, inner), half(count, inner)],
        [upstream, middle, own, other, *pieces, context, shares],
        [None] * 4 + [spec((width // PIECES, inner), 0, 1)] * PIECES + [None] * 2,
        scratch=[pltpu.VMEM((count, inner), jnp.float32)],
    )


def attend_back_shares(query, keys, values, grad_context, shares, grad_values, cosine, sine, query_keys, values_out):
    count, inner = query.shape
    width = query_keys[0].shape[0] * PIECES
    tiles = list(tiles_of(count, inner))

    def body(query_ref, keys_ref, values_ref, grad_context_ref, shares_ref, grad_values_ref, cosine_ref, sine_ref,
             a, b, c, d, e, f, g, h, grad_ref, back_ref, total_ref):
        total_ref[...] = jnp.zeros_like(total_ref)
        cosine, sine = cosine_ref[...], sine_ref[...]
        for number, pair, queries, window in tiles:
            upper = both_heads(grad_context_ref[queries, group(pair)])
            grad_shares = product(values_ref[window, group(pair)], upper, NT)
            shares = wide(shares_ref[number])
            sums = jnp.sum(shares * grad_shares, axis=0, keepdims=True)
            grad_scores = low(shares * (grad_shares - sums))
            grad_query = one_pair(product(grad_scores, keys_ref[window, group(pair)], TN)) * SCALE
            grad_query = grad_query * cosine[queries] - partner(grad_query) * sine[queries]
            grad_ref[queries, group(pair)] = low(grad_query)
            lower = both_heads(query_ref[queries, group(pair)])
            total_ref[window, group(pair)] += product(grad_scores, lower)
        for pair in range(inner // LANES):
            grad_keys = total_ref[:, group(pair)] * SCALE
            grad_keys = grad_keys * cosine - partner(grad_keys) * sine
            grad_ref[:, group(pair + inner // LANES)] = low(grad_keys)
        back = product(grad_ref[...], rows_of((a, b, c, d)), NT)
        back_ref[...] = low(back + product(grad_values_ref[...], rows_of((e, f, g, h)), NT))

    return run(
        body,
        [half(count, 2 * inner), half(count, width)],
        [query, keys, values, grad_context, shares, grad_values, cosine, sine, *query_keys, *values_out],
        [None] * (8 + PIECES) + [spec((width // PIECES, inner), 0, 0)] * PIECES,
        scratch=[pltpu.VMEM((count, inner), jnp.float32)],
    )


def paired_grads(groups):
    pairs = [pair for group in groups for pair in group]
    count, width = pairs[0][0].shape
    sizes = [sum(right.shape[1] for _, right in group) for group in groups]

    def body(*refs):
        outs, number = refs[2 * len(pairs) :], 0
        for i, group in enumerate(groups):
            start = 0
            for _, right in group:
                size = right.shape[1]
                for side in range(2):
                    part = slice(side * width // 2, (side + 1) * width // 2)
                    both = product(refs[2 * number][:, part], refs[2 * number + 1][...], TN)
                    outs[2 * i + side][:, start : start + size] = low(both)
                start += size
                number += 1

    return run(
        body,
        [half(width // 2, size) for size in sizes for _ in range(2)],
        [array for pair in pairs for array in pair],
    )


def input_grads(branch, inputs, own, other, order):
    count, width = inputs.shape

    def body(branch_ref, inputs_ref, own_ref, other_ref, order_ref, out_ref):
        normed, inverse = normalize(wide(inputs_ref[...]))
        scaled = wide(own_ref[...]) + wide(other_ref[...])
        total = wide(branch_ref[...]) + norm_back(scaled, normed, inverse)
        out_ref[...] = product(low(total), order_ref[...])

    return run(
        body,
        [full(count, width)],
        [branch, inputs, own, other, order],
        last=True,
    )[0]


def rope_tables(positions):
    frequency = THETA ** (-jnp.arange(0, HD, 2).astype(jnp.float32) / HD)
    angle = positions.astype(jnp.float32)[:, None] * jnp.tile(frequency, LANES // (HD // 2))[None, :]
    sign = jnp.where(jnp.arange(LANES) % HD < HD // 2, -1.0, 1.0)
    return jnp.cos(angle), jnp.sin(angle) * sign[None, :]


def padded(values, width):
    return jnp.pad(values, ((0, 0), (0, width - values.shape[1])))


def per_device(
    devices, tokens, seg_ids, positions, gain_attn, w_qkv, w_attn_out, gain_mlp, w_in, w_mlp_out, cotangent
):
    width = tokens.shape[1]
    rows, _, inner = w_qkv.shape
    hidden = w_in.shape[2]
    room = -(-hidden // LANES) * LANES
    gain_one, gain_two = wide(gain_attn)[:, None], wide(gain_mlp)[:, None]
    scaled_qkv = [low(wide(w_qkv[:, i]) * gain_one) for i in range(3)]
    scaled_in = [padded(low(wide(w_in[:, i]) * gain_two), room) for i in range(2)]
    shard_one = jnp.concatenate(scaled_qkv[:2], axis=1)
    shard_two = jnp.concatenate([scaled_qkv[2], w_attn_out.T], axis=1)
    shard_three = jnp.concatenate(scaled_in, axis=1)
    shard_four = padded(w_mlp_out.T, room)
    latest.clear()
    query_keys = Gather(shard_one, devices)
    down = Gather(shard_four, devices, late=True)
    order, back = placement(devices, width)
    cosine, sine = rope_tables(positions)
    column, row = seg_ids[:, None], seg_ids[None, :]
    held = query_keys.stack()
    values_out = Gather(after(shard_two, held), devices)
    inputs, normed_one = prepare(tokens, order)
    wait_for(query_keys.other, query_keys.pieces[2])
    held = values_out.stack()
    gates_in = Gather(after(shard_three, held), devices, tail=True)
    wait_for(cosine, sine, column)
    down.join_rows()
    query, keys, shares = attend_shares(normed_one, query_keys.pieces, cosine, sine, column, row)
    wait_for(values_out.other)
    held = gates_in.stack(WEIGHT)
    down.begin(held)
    values, context, own = attend_values(normed_one, values_out.pieces, shares)
    other = swapped(own)
    gains = jnp.concatenate([gain_two, gain_one], axis=1)

    upstream = reorder(cotangent, order)
    down.stack()
    gates_in.share(gates_in.other)
    middle, normed_two = settle(inputs, own, other)
    mixed, grad_gates, own_out, own_two = feed_forward(
        normed_two, upstream, gates_in.pieces, down.pieces
    )
    other_two = swapped(own_two)
    grads_mlp = feed_forward_grads(normed_two, mixed, grad_gates, upstream)
    sums_mlp = Scatter(grads_mlp[:3], grads_mlp[3:], devices, rows)
    sums_mlp.second()
    early = own_out.shape[0] // EARLY
    upper_out = swapped(own_out[:early])
    branch, grad_context, grad_values = attend_back_values(
        upstream, middle, own_two, other_two, values_out.pieces, context, shares
    )
    grad_query_keys, own_one = attend_back_shares(
        query, keys, values, grad_context, shares, grad_values, cosine, sine, query_keys.pieces, values_out.pieces
    )
    other_one = swapped(own_one)
    wait_for(upper_out, *sums_mlp.other)
    kept, sent = paired_grads(
        [[(normed_one, grad_query_keys), (normed_one, grad_values), (branch, context)]]
    )
    sums = Scatter([kept], [sent], devices, rows)
    sums_mlp.third()
    sums.second()
    sum_mlp = add_all(sums_mlp.parts)
    sums.third()
    lower_out = swapped(after(own_out[early:], sum_mlp))
    columns = gain_columns(sum_mlp, shard_three, gains)
    grad_input = input_grads(branch, inputs, own_one, other_one, back)
    output = add_output(middle, own_out, (upper_out, lower_out), back)
    sum_qkv, sum_out, share = finish_attention(sums.parts, shard_one, shard_two, columns)
    sum_in, sum_down = finish_feed_forward(sum_mlp, gains, hidden)
    gains = after(share, sum_down) + swapped(share)
    sum_qkv = jnp.transpose(sum_qkv, (1, 0, 2))
    return (output, grad_input, gains[0], sum_qkv, sum_out.T, gains[1], sum_in, sum_down.T)


def solution(mesh):
    return jax.shard_map(
        functools.partial(per_device, mesh.shape["dp"]),
        mesh=mesh,
        in_specs=(
            P("dp", None),
            P("dp"),
            P("dp"),
            P("dp"),
            P("dp", None, "tensor"),
            P("tensor", "dp"),
            P("dp"),
            P("dp", None, "tensor"),
            P("tensor", "dp"),
            P("dp", None),
        ),
        out_specs=(
            P("dp", None),
            P("dp", None),
            P("dp"),
            P("dp", None, "tensor"),
            P("tensor", "dp"),
            P("dp"),
            P("dp", None, "tensor"),
            P("tensor", "dp"),
        ),
        check_vma=False,
    )
```
